512 devices in a mesh: grp: 8 (over z_lo, x), ep: 64 (over z_hi, y, core).
Axes of the slice: x: 4, y: 8, z: 8 (z_hi: 4, z_lo: 2; z = z_hi * 2 + z_lo), core: 2. Of those that a mesh axis runs over, the one named last changes fastest.
Arguments:
- latent_cache: bfloat16 [8, 64, 4, 64, 576], P('grp', 'ep'), may hold values from -6 to 6
- page_table: int32 [8, 64, 2, 2], P('grp', 'ep'), may hold values from 0 to 3, as said below
- lengths: int32 [8, 64, 2], P('grp', 'ep'), may hold values from 1 to 128, as said below
- move_to: int32 [8, 64, 2], P('grp', 'ep'), may hold values from 0 to 2, as said below
- query: bfloat16 [8, 64, 2, 64, 576], P('grp', 'ep'), may hold values from -110 to 110
- hidden: bfloat16 [8, 64, 2, 3584], P('grp', 'ep'), may hold values from -6 to 6
- norm_gain: float32 [3584], replicated, may hold values from 0.1 to 1.9
- expert_ids: int32 [8, 64, 4, 6], P('grp', 'ep'), may hold values from 0 to 7, all different within a row; in each aligned block of 4 rows (0 to 3, 4 to 7, ..., all dimensions but the last counted through in order) at most 4 rows name the same one
- expert_gates: float32 [8, 64, 4, 6], P('grp', 'ep'), may hold values from 0.05 to 1
- gate_weight: bfloat16 [64, 3584, 128], P('ep'), may hold values from -0.09375 to 0.09375
- up_weight: bfloat16 [64, 3584, 128], P('ep'), may hold values from -0.09375 to 0.09375
- down_weight: bfloat16 [64, 128, 3584], P('ep'), may hold values from -0.1875 to 0.1875
Outputs:
- attn_out: bfloat16 [8, 64, 4, 64, 512], P('grp', 'ep')
- moe_out: bfloat16 [8, 64, 4, 3584], P('grp', 'ep')
The draws below stay inside these ranges and needn't reach their ends.
Inputs may be any that keep to these rules, and one draw needn't show every extreme that they name: `page_table`: each device's table holds each of its 4 pages once. `lengths`: some request has exactly 128 tokens. `move_to`: on one device each of the values 1 and 2 is named by at most one request. `expert_ids`: among the rows of one device no expert is named by more than 4 rows.
All inputs are finite; a program needn't handle non-finite values.
Results may differ from the reference program's by a relative error of at most 0.014.
Values may be sent and summed in bfloat16 or wider, within the bound.
No kernel may reach another device: no remote copies, remote signals or barrier semaphores. Data moves between devices by JAX's collectives and lax.ppermute only.
A program may use at most 64 MiB of HBM per device.

```python
import math
import jax
import jax.numpy as jnp
import numpy as np
from jax import lax

D = 3584
HEADS = 64
LAT = 576
VDIM = 512
QK_DIM = 192
PAGE = 64
MAXP = 2
FF = 1024
SLICES = 8
REQ = 2
POOL = 4
SERVE = 4
EXP_WIN = 8
TOP_WIN = 6
CAP = 4
N_GRP = 8
N_EP = 64


def draw_page_table(key, part):
    key = jax.random.fold_in(key, 11)
    scores = jax.random.randint(key, (N_GRP, N_EP, POOL), 0, POOL)
    ranked = scores * POOL + jnp.arange(POOL, dtype=jnp.int32)
    order = jnp.argsort(ranked, axis=-1, stable=True).astype(jnp.int32)
    return order.reshape(N_GRP, N_EP, REQ, MAXP)


def load_plan(key):
    plan_key = jax.random.fold_in(key, 40)
    keys = jax.random.split(plan_key, 3)
    shape = (N_GRP, N_EP)
    busy = jax.random.randint(keys[0], shape, 0, 2)
    first_device = (jnp.arange(N_GRP * N_EP, dtype=jnp.int32) == 0).reshape(shape)
    busy = jnp.where(first_device, 1, busy)
    double = jax.random.randint(keys[1], shape, 0, 2)
    scores = jax.random.randint(keys[2], shape + (REQ,), 0, REQ) * REQ + jnp.arange(REQ, dtype=jnp.int32)
    ranks = jnp.argsort(jnp.argsort(scores, axis=-1, stable=True), axis=-1, stable=True).astype(jnp.int32)
    return (busy, double, ranks)


def draw_lengths(key, part):
    busy, double, ranks = load_plan(key)
    key = jax.random.fold_in(key, 12)
    first_key, second_key = jax.random.split(key)
    longest_len = MAXP * PAGE
    shape = (N_GRP, N_EP, REQ)
    heavy = jax.random.randint(first_key, shape, max(longest_len // 2, 1), longest_len + 1)
    light = jax.random.randint(second_key, shape, 1, PAGE + 1)
    heavy = jnp.where(ranks == 0, longest_len, heavy)
    return jnp.where(busy[..., None] == 1, heavy, light).astype(jnp.int32)


def draw_move_to(key, part):
    busy, double, ranks = load_plan(key)
    loaded = busy[..., None] == 1
    moved = jnp.where(loaded & (ranks == 0), 1, 0)
    moved = jnp.where(loaded & (double[..., None] == 1) & (ranks == 1), 2, moved)
    return moved.astype(jnp.int32)


def draw_query(key, part):
    key = jax.random.fold_in(key, 14)
    first_key = jax.random.fold_in(key, 0)
    shape = (N_GRP, N_EP, REQ, HEADS, LAT)
    values = jnp.clip(jax.random.normal(first_key, shape, jnp.float32), -6.0, 6.0)
    return values.astype(jnp.bfloat16)


def steps_of(rng, extent, cuts, smallest, high):
    loudness, own = 1.0, jax.random.fold_in(rng, 6)
    for axis_at, shards_of in cuts:
        steps = jnp.exp(jax.random.uniform(jax.random.fold_in(own, axis_at), (shards_of,), jnp.float32, smallest / len(cuts), high / len(cuts)))
        loudness = loudness * jnp.repeat(steps, extent[axis_at] // shards_of).reshape([-1 if axis == axis_at else 1 for axis in range(len(extent))])
    return loudness


def assign_block(key, own, number, rows, amount, top, most, lean):
    order = jax.random.permutation(key, amount)
    packed, common = shares(amount, rows * top, most, lean, True), shares(amount, rows * top, most, lean, False)
    places = jnp.arange(amount)

    def named(sizes, turn):
        used = int((sizes > 0).sum())
        fixed = max(1, used // 4)
        moved = fixed + (places - fixed + turn * (used - fixed)) % max(1, amount - fixed)
        return jnp.zeros((amount,), jnp.int32).at[order[jnp.where(places < fixed, places, moved)]].set(jnp.asarray(sizes, jnp.int32))

    sizes = jnp.where(number % 4 == 0, named(packed, number // 4), named(common, number - number // 4 - 1))
    mixed = jax.random.permutation(jax.random.fold_in(own, 3), amount)
    giver, sink = mixed[0:amount // 2 * 2:2], mixed[1:amount // 2 * 2:2]
    margin = jnp.minimum(sizes[giver] - 1, most - sizes[sink]) // 2
    margin = jnp.where((giver == order[0]) | (sink == order[0]) | (sizes[sink] == 0), 0, jnp.maximum(margin, 0))
    moved = jax.random.randint(jax.random.fold_in(own, 4), (amount // 2,), 0, 1 << 20) % (margin + 1)
    sizes = sizes.at[giver].add(-moved).at[sink].add(moved)
    members = jnp.searchsorted(jnp.cumsum(sizes), jnp.arange(rows * top), side="right").astype(jnp.int32)
    listing = members.reshape(top, rows).T
    listing = listing[jax.random.permutation(jax.random.fold_in(own, 1), rows)]
    turn = jax.random.randint(jax.random.fold_in(own, 2), (rows, 1), 0, top)
    return jnp.take_along_axis(listing, (jnp.arange(top)[None, :] + turn) % top, axis=1)


def shares(number_of, total, most, skew, full):
    loads = [(1 << 20) // math.isqrt(grade ** skew) + 1 for grade in range(1, number_of + 1)]
    largest = most if full else min(most, max(-(-total // number_of), total * loads[0] // sum(loads)))
    least = 1 if total - largest >= number_of - 1 else 0
    given, spare = [largest] + [least] * (number_of - 1), total - largest - least * (number_of - 1)
    while spare > 0:
        candidates = [i for i in range(1, number_of) if given[i] < largest] or [i for i in range(1, number_of) if given[i] < most]
        whole, budget = sum([loads[i] for i in candidates]), spare
        for i in candidates:
            more = min(most - given[i], max(1, budget * loads[i] // whole), spare)
            given[i] = given[i] + more
            spare = spare - more
    return np.array(given)


def gaussian(rng, dims, width, reach, cuts=(), kind=jnp.bfloat16):
    entries = width * jax.random.normal(rng, dims, jnp.float32)
    if cuts:
        entries = entries * steps_of(rng, dims, cuts, -0.22, 0.18)
    return jnp.clip(entries, -reach, reach).astype(kind)


def setup_inputs(seed: int = 0) -> dict:
    key_list = jax.random.split(jax.random.key(seed), 13)
    latent_cache = gaussian(key_list[0], (N_GRP, N_EP, POOL, PAGE, LAT), 1.0, 6.0, ((0, 8), (1, 64)))
    page_table = draw_page_table(jax.random.fold_in(key_list[12], 71), 0)
    lengths = draw_lengths(jax.random.fold_in(key_list[12], 71), 0)
    move_to = draw_move_to(jax.random.fold_in(key_list[12], 71), 0)
    query = draw_query(jax.random.fold_in(key_list[12], 71), 0)
    hidden = gaussian(key_list[5], (N_GRP, N_EP, REQ, D), 1.0, 6.0, ((0, 8), (1, 64)))
    norm_gain = jnp.clip(1.0 + 0.18 * jax.random.normal(key_list[6], (D,), jnp.float32), 0.1, 1.9)
    expert_ids_keys = jax.random.split(jax.random.fold_in(key_list[7], 1), N_GRP * N_EP * SERVE // SERVE)
    expert_ids_turns = jax.random.permutation(jax.random.fold_in(key_list[7], 3), N_GRP * N_EP * SERVE // SERVE)
    expert_ids = jax.vmap(lambda own, number: assign_block(jax.random.fold_in(key_list[7], 2), own, number, SERVE, EXP_WIN, TOP_WIN, CAP, 2))(expert_ids_keys, expert_ids_turns).reshape((N_GRP, N_EP, SERVE, TOP_WIN))
    expert_gates = jnp.clip(jnp.exp(math.log(1.0) - 2.9957323 * jax.random.uniform(key_list[8], (N_GRP, N_EP, SERVE, TOP_WIN), jnp.float32) ** steps_of(key_list[8], (N_GRP, N_EP, SERVE, TOP_WIN), ((0, 8), (1, 64)), -0.2, 0.2)), 0.05, 1.0)
    gate_weight = gaussian(key_list[9], (N_EP, D, FF // SLICES), D ** -0.5, 0.09375, ((0, 64),))
    up_weight = gaussian(key_list[10], (N_EP, D, FF // SLICES), D ** -0.5, 0.09375, ((0, 64),))
    down_weight = gaussian(key_list[11], (N_EP, FF // SLICES, D), FF ** -0.5, 0.1875, ((0, 64),))
    return {"latent_cache": latent_cache, "page_table": page_table, "lengths": lengths, "move_to": move_to, "query": query, "hidden": hidden, "norm_gain": norm_gain, "expert_ids": expert_ids, "expert_gates": expert_gates, "gate_weight": gate_weight, "up_weight": up_weight, "down_weight": down_weight}


def request_attention(pool, table, question, length):
    keys = pool[table].reshape(MAXP * PAGE, LAT)
    scores = jnp.dot(question, keys.T, preferred_element_type=jnp.float32) * QK_DIM ** (-0.5)
    live = jnp.arange(MAXP * PAGE) < length
    scores = jnp.where(live[None, :], scores, jnp.float32(-1e+30))
    top = lax.optimization_barrier(jnp.max(scores, axis=1, keepdims=True))
    expo = jnp.exp(scores - top)
    probs = (expo / lax.optimization_barrier(jnp.sum(expo, axis=1, keepdims=True))).astype(jnp.bfloat16)
    return jnp.dot(probs, keys[:, :VDIM], preferred_element_type=jnp.float32)

def arrive(move_to, values):
    wide = values.astype(jnp.float32)
    forward = (move_to == 1).astype(jnp.float32)
    backward = (move_to == 2).astype(jnp.float32)
    from_prev = jnp.roll(jnp.einsum('gej,gej...->ge...', forward, wide), 1, axis=0)
    from_next = jnp.roll(jnp.einsum('gej,gej...->ge...', backward, wide), -1, axis=0)
    stays = move_to == 0
    extra = (1,) * (values.ndim - 3)
    local = jnp.where(stays.reshape(stays.shape + extra), values, jnp.zeros_like(values))
    return jnp.concatenate([local, from_prev[:, :, None].astype(values.dtype), from_next[:, :, None].astype(values.dtype)], axis=2)

def reference(latent_cache, page_table, lengths, move_to, query, hidden, norm_gain, expert_ids, expert_gates, gate_weight, up_weight, down_weight):
    devices = N_GRP * N_EP

    def device_block(inputs):
        pool, table, questions, lens = inputs
        return jax.vmap(lambda t, q, l: request_attention(pool, t, q, l))(table, questions, lens)
    attention = lax.map(device_block, (latent_cache.reshape((devices,) + latent_cache.shape[2:]), page_table.reshape((devices,) + page_table.shape[2:]), query.reshape((devices,) + query.shape[2:]), lengths.reshape((devices,) + lengths.shape[2:])))
    attention = attention.reshape(N_GRP, N_EP, REQ, HEADS, VDIM).astype(jnp.bfloat16)
    attn_out = arrive(move_to, attention)
    served = arrive(move_to, hidden).astype(jnp.float32)
    normed = (served * lax.rsqrt(lax.optimization_barrier(jnp.mean(served * served, axis=-1, keepdims=True)) + 1e-06) * norm_gain.astype(jnp.float32)).astype(jnp.bfloat16)
    onehot = (expert_ids[..., None] == jnp.arange(EXP_WIN, dtype=jnp.int32)).astype(jnp.float32)
    chosen = lax.optimization_barrier(jnp.sum(onehot, axis=3))
    slot = jnp.cumsum(chosen, axis=2) - chosen
    place = chosen[..., None] * (slot[..., None] == jnp.arange(CAP, dtype=jnp.float32)).astype(jnp.float32)
    buffers = jnp.einsum('gesxc,gesd->gexcd', place, normed.astype(jnp.float32)).astype(jnp.bfloat16)

    def expert_block(index):
        group_id = index // EXP_WIN
        expert_id = index % EXP_WIN
        rows = buffers[group_id, :, expert_id].reshape(N_EP * CAP, D)

        def one_part(total, part_id):
            which = expert_id * SLICES + part_id
            gate = jnp.dot(rows, gate_weight[which], preferred_element_type=jnp.float32)
            upper = jnp.dot(rows, up_weight[which], preferred_element_type=jnp.float32)
            act = (jax.nn.silu(gate) * upper).astype(jnp.bfloat16)
            part = jnp.dot(act, down_weight[which], preferred_element_type=jnp.float32).astype(jnp.bfloat16)
            return (total + part.astype(jnp.float32), None)
        total, _ = lax.scan(one_part, jnp.zeros((N_EP * CAP, D), jnp.float32), jnp.arange(SLICES, dtype=jnp.int32))
        return total.reshape(N_EP, CAP, D)
    expert_out = lax.map(expert_block, jnp.arange(N_GRP * EXP_WIN, dtype=jnp.int32))
    expert_out = expert_out.reshape(N_GRP, EXP_WIN, N_EP, CAP, D)
    mix = jnp.einsum('gesk,geskx->gesx', expert_gates.astype(jnp.float32), onehot)
    weights = mix[..., None] * place
    moe_out = jnp.einsum('gesxc,gxecd->gesd', weights, expert_out).astype(jnp.bfloat16)
    return (attn_out, moe_out)
```

```python
import jax
import jax.numpy as jnp
from jax import lax
from jax.sharding import PartitionSpec as P

VDIM = 512
QK_DIM = 192
SLICES = 8


def passed_along(shard, axis, by):
    length = lax.axis_size(axis)
    return lax.ppermute(shard, axis, [(i, (i + by) % length) for i in range(length)])


def attend_rows(questions, keys, lens):
    scores = jnp.einsum(
        "rhl,rtl->rht", questions, keys, preferred_element_type=jnp.float32
    ) * QK_DIM ** (-0.5)
    live = jnp.arange(keys.shape[1], dtype=jnp.int32)[None, None, :] < lens[:, None, None]
    scores = jnp.where(live, scores, jnp.float32(-1e30))
    top = jnp.max(scores, axis=2, keepdims=True)
    expo = jnp.exp(scores - top)
    probs = (expo / jnp.sum(expo, axis=2, keepdims=True)).astype(jnp.bfloat16)
    out = jnp.einsum("rht,rtv->rhv", probs, keys[:, :, :VDIM], preferred_element_type=jnp.float32)
    return out.astype(jnp.bfloat16)


def body(
    latent_cache,
    page_table,
    lengths,
    move_to,
    query,
    hidden,
    norm_gain,
    expert_ids,
    expert_gates,
    gate_weight,
    up_weight,
    down_weight,
):
    pool = latent_cache[0, 0]
    table = page_table[0, 0]
    requests = table.shape[0]
    moves = move_to[0, 0]
    rows = hidden[0, 0]
    width = rows.shape[1]
    devices = lax.axis_size("ep")
    experts_here = devices // SLICES

    onehot = (
        expert_ids[0, 0][:, :, None] == jnp.arange(experts_here, dtype=jnp.int32)
    ).astype(jnp.float32)
    mix = jnp.einsum("sk,skx->sx", expert_gates[0, 0], onehot, precision=lax.Precision.HIGHEST)
    mix_next = passed_along(mix[requests : requests + 1], "grp", -1)
    mix_prev = passed_along(mix[requests + 1 : requests + 2], "grp", 1)
    at = moves[:, None]
    mix_home = jnp.where(
        at == 0, mix[:requests], jnp.where(at == 1, mix_next, mix_prev)
    )

    wide = rows.astype(jnp.float32)
    normed = (
        wide * lax.rsqrt(jnp.mean(wide * wide, axis=-1, keepdims=True) + 1e-06) * norm_gain
    ).astype(jnp.bfloat16)
    outgoing = jnp.broadcast_to(normed[None], (devices, requests, width))
    received = lax.all_to_all(outgoing, "ep", split_axis=0, concat_axis=0, tiled=True)
    flat = received.reshape(devices * requests, width)
    gate = jnp.dot(flat, gate_weight[0], preferred_element_type=jnp.float32)
    upper = jnp.dot(flat, up_weight[0], preferred_element_type=jnp.float32)
    act = (jax.nn.silu(gate) * upper).astype(jnp.bfloat16)
    part = jnp.dot(act, down_weight[0], preferred_element_type=jnp.float32).astype(jnp.bfloat16)
    returned = lax.all_to_all(
        part.reshape(devices, requests, width), "ep", split_axis=0, concat_axis=0, tiled=True
    )
    summed = jnp.sum(
        returned.reshape(experts_here, SLICES, requests, width).astype(jnp.float32), axis=1
    )
    moe = jnp.sum(summed * mix_home.T[:, :, None], axis=0).astype(jnp.bfloat16)

    keys = pool[table.reshape(-1)].reshape(requests, table.shape[1] * pool.shape[1], pool.shape[2])
    attn = attend_rows(query[0, 0], keys, lengths[0, 0])
    heads = attn.shape[1]
    both = jnp.concatenate([attn, moe.reshape(requests, width // VDIM, VDIM)], axis=1)

    def picked(which):
        keep = (moves == which)[:, None, None]
        return jnp.sum(jnp.where(keep, both, jnp.zeros_like(both)), axis=0, dtype=jnp.bfloat16)

    from_prev = passed_along(picked(1), "grp", 1)
    from_next = passed_along(picked(2), "grp", -1)
    stay = jnp.where((moves == 0)[:, None, None], both, jnp.zeros_like(both))
    served = jnp.concatenate([stay, from_prev[None], from_next[None]], axis=0)
    return (
        served[None, None, :, :heads],
        served[:, heads:].reshape(1, 1, served.shape[0], width),
    )


def solution(mesh):
    in_specs = (
        P("grp", "ep", None, None, None),
        P("grp", "ep", None, None),
        P("grp", "ep", None),
        P("grp", "ep", None),
        P("grp", "ep", None, None, None),
        P("grp", "ep", None, None),
        P(),
        P("grp", "ep", None, None),
        P("grp", "ep", None, None),
        P("ep", None, None),
        P("ep", None, None),
        P("ep", None, None),
    )
    out_specs = (P("grp", "ep", None, None, None), P("grp", "ep", None, None))
    return jax.shard_map(body, mesh=mesh, in_specs=in_specs, out_specs=out_specs, check_vma=False)
```

```python
import jax
import jax.numpy as jnp
from jax import lax
from jax.sharding import PartitionSpec as P

VDIM = 512
QK_DIM = 192
SLICES = 8


def passed_along(shard, axis, by):
    length = lax.axis_size(axis)
    return lax.ppermute(shard, axis, [(i, (i + by) % length) for i in range(length)])


def attend_rows(questions, keys, lens):
    scores = jnp.einsum(
        "rhl,rtl->rht", questions, keys, preferred_element_type=jnp.float32
    ) * QK_DIM ** (-0.5)
    live = jnp.arange(keys.shape[1], dtype=jnp.int32)[None, None, :] < lens[:, None, None]
    scores = jnp.where(live, scores, jnp.float32(-1e30))
    top = jnp.max(scores, axis=2, keepdims=True)
    expo = jnp.exp(scores - top)
    probs = (expo / jnp.sum(expo, axis=2, keepdims=True)).astype(jnp.bfloat16)
    out = jnp.einsum("rht,rtv->rhv", probs, keys[:, :, :VDIM], preferred_element_type=jnp.float32)
    return out.astype(jnp.bfloat16)


def body(
    latent_cache,
    page_table,
    lengths,
    move_to,
    query,
    hidden,
    norm_gain,
    expert_ids,
    expert_gates,
    gate_weight,
    up_weight,
    down_weight,
):
    pool = latent_cache[0, 0]
    table = page_table[0, 0]
    requests = table.shape[0]
    moves = move_to[0, 0]
    rows = hidden[0, 0]
    width = rows.shape[1]
    devices = lax.axis_size("ep")
    experts_here = devices // SLICES

    onehot = (
        expert_ids[0, 0][:, :, None] == jnp.arange(experts_here, dtype=jnp.int32)
    ).astype(jnp.float32)
    mix = jnp.einsum("sk,skx->sx", expert_gates[0, 0], onehot, precision=lax.Precision.HIGHEST)
    mix_next = passed_along(mix[requests : requests + 1], "grp", -1)
    mix_prev = passed_along(mix[requests + 1 : requests + 2], "grp", 1)
    at = moves[:, None]
    mix_home = jnp.where(
        at == 0, mix[:requests], jnp.where(at == 1, mix_next, mix_prev)
    )

    keys = pool[table.reshape(-1)].reshape(requests, table.shape[1] * pool.shape[1], pool.shape[2])
    attn = attend_rows(query[0, 0], keys, lengths[0, 0])

    def picked(which, values):
        keep = (moves == which).reshape((requests,) + (1,) * (values.ndim - 1))
        return jnp.sum(jnp.where(keep, values, jnp.zeros_like(values)), axis=0, dtype=values.dtype)

    def served(values, from_prev, from_next):
        keep = (moves == 0).reshape((requests,) + (1,) * (values.ndim - 1))
        stay = jnp.where(keep, values, jnp.zeros_like(values))
        return jnp.concatenate([stay, from_prev[None], from_next[None]], axis=0)

    attn_prev = passed_along(picked(1, attn), "grp", 1)
    attn_next = passed_along(picked(2, attn), "grp", -1)

    wide = rows.astype(jnp.float32)
    normed = (
        wide * lax.rsqrt(jnp.mean(wide * wide, axis=-1, keepdims=True) + 1e-06) * norm_gain
    ).astype(jnp.bfloat16)
    chips = devices // requests
    outgoing = jnp.broadcast_to(normed[None], (chips, requests, width)).reshape(devices, 1, width)
    received = lax.all_to_all(outgoing, "ep", split_axis=0, concat_axis=0, tiled=True)
    received, attn_prev, attn_next, mix_home = lax.optimization_barrier(
        (received, attn_prev, attn_next, mix_home)
    )
    swap = [(i, i ^ 1) for i in range(devices)]
    mine = received.reshape(devices, width)
    theirs = lax.ppermute(mine, "ep", swap)

    def experts(values):
        gate = jnp.dot(values, gate_weight[0], preferred_element_type=jnp.float32)
        upper = jnp.dot(values, up_weight[0], preferred_element_type=jnp.float32)
        act = (jax.nn.silu(gate) * upper).astype(jnp.bfloat16)
        return jnp.dot(act, down_weight[0], preferred_element_type=jnp.float32)

    part_theirs = experts(theirs).astype(jnp.bfloat16)
    part_mine = experts(mine)
    pair = (part_mine + lax.ppermute(part_theirs, "ep", swap).astype(jnp.float32)).astype(jnp.bfloat16)
    returned = lax.all_to_all(
        pair.reshape(devices, 1, width), "ep", split_axis=0, concat_axis=0, tiled=True
    )
    summed = jnp.sum(
        returned.reshape(experts_here, SLICES // requests, requests, width).astype(jnp.float32), axis=1
    )
    moe = jnp.sum(summed * mix_home.T[:, :, None], axis=0).astype(jnp.bfloat16)
    moe_prev = passed_along(picked(1, moe), "grp", 1)
    moe_next = passed_along(picked(2, moe), "grp", -1)
    return (
        served(attn, attn_prev, attn_next)[None, None],
        served(moe, moe_prev, moe_next)[None, None],
    )


def solution(mesh):
    in_specs = (
        P("grp", "ep", None, None, None),
        P("grp", "ep", None, None),
        P("grp", "ep", None),
        P("grp", "ep", None),
        P("grp", "ep", None, None, None),
        P("grp", "ep", None, None),
        P(),
        P("grp", "ep", None, None),
        P("grp", "ep", None, None),
        P("ep", None, None),
        P("ep", None, None),
        P("ep", None, None),
    )
    out_specs = (P("grp", "ep", None, None, None), P("grp", "ep", None, None))
    return jax.shard_map(body, mesh=mesh, in_specs=in_specs, out_specs=out_specs, check_vma=False)
```

```python
import jax
import jax.numpy as jnp
from jax import lax
from jax.experimental import pallas as pl
from jax.experimental.pallas import tpu as pltpu
from jax.sharding import PartitionSpec as P

VDIM = 512
QK_DIM = 192
SLICES = 8


def passed_along(shard, axis, by):
    length = lax.axis_size(axis)
    return lax.ppermute(shard, axis, [(i, (i + by) % length) for i in range(length)])


def attend_rows(questions, keys, lens):
    scores = jnp.einsum(
        "rhl,rtl->rht", questions, keys, preferred_element_type=jnp.float32
    ) * QK_DIM ** (-0.5)
    live = jnp.arange(keys.shape[1], dtype=jnp.int32)[None, None, :] < lens[:, None, None]
    scores = jnp.where(live, scores, jnp.float32(-1e30))
    top = jnp.max(scores, axis=2, keepdims=True)
    expo = jnp.exp(scores - top)
    probs = (expo / jnp.sum(expo, axis=2, keepdims=True)).astype(jnp.bfloat16)
    out = jnp.einsum("rht,rtv->rhv", probs, keys[:, :, :VDIM], preferred_element_type=jnp.float32)
    return out.astype(jnp.bfloat16)


def columns_of(ref, which, size):
    return ref[:, pl.ds(pl.multiple_of(which * size, 128), size)]


def dot(left, right):
    return jnp.dot(left, right, preferred_element_type=jnp.float32)


def experts_kernel(core, x, gain, w_gate, w_up, w_down, act, part):
    rows, half = x.shape[0] // 2, x.shape[1]
    low = x[:rows].astype(jnp.float32)
    high = x[rows:].astype(jnp.float32)
    square = jnp.sum(low * low, axis=1, keepdims=True) + jnp.sum(high * high, axis=1, keepdims=True)
    scale = lax.rsqrt(square / (2 * half) + 1e-06)
    low = (low * scale * gain[:, :half]).astype(jnp.bfloat16)
    high = (high * scale * gain[:, half:]).astype(jnp.bfloat16)
    gate = dot(low, w_gate[:half]) + dot(high, w_gate[half:])
    upper = dot(low, w_up[:half]) + dot(high, w_up[half:])
    hidden_units = (jax.nn.silu(gate) * upper).astype(jnp.bfloat16)
    act[...] = hidden_units
    part[...] = dot(hidden_units, columns_of(w_down, 1 - core[0], half)).astype(jnp.bfloat16)


def join_kernel(core, act, other, w_down, pair):
    half = other.shape[1]
    mine = dot(act[...], columns_of(w_down, core[0], half))
    pair[...] = (mine + other[...].astype(jnp.float32)).astype(jnp.bfloat16)


def in_vmem(count):
    return [pl.BlockSpec(memory_space=pltpu.SMEM)] + [
        pl.BlockSpec(memory_space=pltpu.VMEM) for _ in range(count)
    ]


LIMIT = pltpu.CompilerParams(vmem_limit_bytes=24 * 1024 * 1024)


def body(
    latent_cache,
    page_table,
    lengths,
    move_to,
    query,
    hidden,
    norm_gain,
    expert_ids,
    expert_gates,
    gate_weight,
    up_weight,
    down_weight,
):
    pool = latent_cache[0, 0]
    table = page_table[0, 0]
    requests = table.shape[0]
    moves = move_to[0, 0]
    rows = hidden[0, 0]
    width = rows.shape[1]
    devices = lax.axis_size("ep")
    experts_here = devices // SLICES

    keys = pool[table.reshape(-1)].reshape(requests, table.shape[1] * pool.shape[1], pool.shape[2])
    attn = attend_rows(query[0, 0], keys, lengths[0, 0])

    def picked(which, values):
        keep = (moves == which).reshape((requests,) + (1,) * (values.ndim - 1))
        return jnp.sum(jnp.where(keep, values, jnp.zeros_like(values)), axis=0, dtype=values.dtype)

    def served(values, from_prev, from_next):
        keep = (moves == 0).reshape((requests,) + (1,) * (values.ndim - 1))
        stay = jnp.where(keep, values, jnp.zeros_like(values))
        return jnp.concatenate([stay, from_prev[None], from_next[None]], axis=0)

    attn_prev = passed_along(picked(1, attn), "grp", 1)
    attn_next = passed_along(picked(2, attn), "grp", -1)

    cores = 2
    half = width // cores
    chips = devices // cores
    halves = rows.reshape(requests, cores, half).transpose(1, 0, 2)
    outgoing = jnp.broadcast_to(halves[None], (chips, cores, requests, half)).reshape(
        devices, requests, half
    )
    received = lax.all_to_all(outgoing, "ep", split_axis=0, concat_axis=0, tiled=True)
    received, attn_prev, attn_next = lax.optimization_barrier((received, attn_prev, attn_next))
    pairs = [[cores * i + j for j in range(cores)] for i in range(chips)]
    swap = [(i, i ^ 1) for i in range(devices)]
    count = devices * requests
    x = lax.all_gather(
        received.reshape(count, half), "ep", axis_index_groups=pairs, axis=0, tiled=True
    )
    core = (lax.axis_index("ep") % cores).astype(jnp.int32).reshape(1)
    w_down = down_weight[0]
    act, part = pl.pallas_call(
        experts_kernel,
        out_shape=(
            jax.ShapeDtypeStruct((count, w_down.shape[0]), jnp.bfloat16),
            jax.ShapeDtypeStruct((count, half), jnp.bfloat16),
        ),
        in_specs=in_vmem(5),
        out_specs=tuple(in_vmem(2)[1:]),
        compiler_params=LIMIT,
    )(core, x, norm_gain[None, :], gate_weight[0], up_weight[0], w_down)
    other = lax.ppermute(part, "ep", swap)
    pair = pl.pallas_call(
        join_kernel,
        out_shape=jax.ShapeDtypeStruct((count, half), jnp.bfloat16),
        in_specs=in_vmem(3),
        out_specs=in_vmem(1)[1],
        compiler_params=LIMIT,
    )(core, act, other, w_down)
    returned = lax.all_to_all(
        pair.reshape(devices, requests, half), "ep", split_axis=0, concat_axis=0, tiled=True
    )

    ids, gates, _ = lax.optimization_barrier((expert_ids[0, 0], expert_gates[0, 0], pair))
    onehot = (
        ids[:, :, None] == jnp.arange(experts_here, dtype=jnp.int32)
    ).astype(jnp.float32)
    mix = jnp.einsum("sk,skx->sx", gates, onehot, precision=lax.Precision.HIGHEST)
    mix_next = passed_along(mix[requests : requests + 1], "grp", -1)
    mix_prev = passed_along(mix[requests + 1 : requests + 2], "grp", 1)
    at = moves[:, None]
    mix_home = jnp.where(
        at == 0, mix[:requests], jnp.where(at == 1, mix_next, mix_prev)
    )


    per_expert = jnp.sum(
        returned.reshape(experts_here, SLICES // cores, cores, requests, half).astype(jnp.float32),
        axis=1,
    )
    mixed = jnp.sum(per_expert * mix_home.T[:, None, :, None], axis=0)
    moe = mixed.transpose(1, 0, 2).reshape(requests, width).astype(jnp.bfloat16)
    moe_prev = passed_along(picked(1, moe), "grp", 1)
    moe_next = passed_along(picked(2, moe), "grp", -1)
    return (
        served(attn, attn_prev, attn_next)[None, None],
        served(moe, moe_prev, moe_next)[None, None],
    )


def solution(mesh):
    in_specs = (
        P("grp", "ep", None, None, None),
        P("grp", "ep", None, None),
        P("grp", "ep", None),
        P("grp", "ep", None),
        P("grp", "ep", None, None, None),
        P("grp", "ep", None, None),
        P(),
        P("grp", "ep", None, None),
        P("grp", "ep", None, None),
        P("ep", None, None),
        P("ep", None, None),
        P("ep", None, None),
    )
    out_specs = (P("grp", "ep", None, None, None), P("grp", "ep", None, None))
    return jax.shard_map(body, mesh=mesh, in_specs=in_specs, out_specs=out_specs, check_vma=False)
```

```python
import jax
import jax.numpy as jnp
from jax import lax
from jax.experimental import pallas as pl
from jax.experimental.pallas import tpu as pltpu
from jax.sharding import PartitionSpec as P

VDIM = 512
QK_DIM = 192
SLICES = 8


def passed_along(shard, axis, by):
    length = lax.axis_size(axis)
    return lax.ppermute(shard, axis, [(i, (i + by) % length) for i in range(length)])


def attend_rows(questions, keys, lens):
    scores = jnp.einsum(
        "rhl,rtl->rht", questions, keys, preferred_element_type=jnp.float32
    ) * QK_DIM ** (-0.5)
    live = jnp.arange(keys.shape[1], dtype=jnp.int32)[None, None, :] < lens[:, None, None]
    scores = jnp.where(live, scores, jnp.float32(-1e30))
    top = jnp.max(scores, axis=2, keepdims=True)
    expo = jnp.exp(scores - top)
    probs = (expo / jnp.sum(expo, axis=2, keepdims=True)).astype(jnp.bfloat16)
    out = jnp.einsum("rht,rtv->rhv", probs, keys[:, :, :VDIM], preferred_element_type=jnp.float32)
    return out.astype(jnp.bfloat16)


def dot(left, right):
    return jnp.dot(left, right, preferred_element_type=jnp.float32)


def share_of(ref, which):
    rows = ref.shape[0] // 2
    return ref[pl.ds(pl.multiple_of(which * rows, 16), rows), :]


def experts_kernel(core, x, gain, w_gate, w_up, w_down, act, part):
    wide = x[...].astype(jnp.float32)
    scale = lax.rsqrt(jnp.mean(wide * wide, axis=1, keepdims=True) + 1e-06)
    normed = (wide * scale * gain[...]).astype(jnp.bfloat16)
    act[...] = (jax.nn.silu(dot(normed, w_gate[...])) * dot(normed, w_up[...])).astype(jnp.bfloat16)
    part[...] = dot(share_of(act, 1 - core[0]), w_down[...]).astype(jnp.bfloat16)


def join_kernel(core, act, parts, w_down, pair):
    mine = dot(share_of(act, core[0]), w_down[...])
    pair[...] = (mine + share_of(parts, 1 - core[0]).astype(jnp.float32)).astype(jnp.bfloat16)


def in_vmem(count):
    return [pl.BlockSpec(memory_space=pltpu.SMEM)] + [
        pl.BlockSpec(memory_space=pltpu.VMEM) for _ in range(count)
    ]


LIMIT = pltpu.CompilerParams(vmem_limit_bytes=24 * 1024 * 1024)


def body(
    latent_cache,
    page_table,
    lengths,
    move_to,
    query,
    hidden,
    norm_gain,
    expert_ids,
    expert_gates,
    gate_weight,
    up_weight,
    down_weight,
):
    pool = latent_cache[0, 0]
    table = page_table[0, 0]
    requests = table.shape[0]
    moves = move_to[0, 0]
    rows = hidden[0, 0]
    width = rows.shape[1]
    devices = lax.axis_size("ep")
    experts_here = devices // SLICES

    keys = pool[table.reshape(-1)].reshape(requests, table.shape[1] * pool.shape[1], pool.shape[2])
    attn = attend_rows(query[0, 0], keys, lengths[0, 0])

    def picked(which, values):
        keep = (moves == which).reshape((requests,) + (1,) * (values.ndim - 1))
        return jnp.sum(jnp.where(keep, values, jnp.zeros_like(values)), axis=0, dtype=values.dtype)

    def served(values, from_prev, from_next):
        keep = (moves == 0).reshape((requests,) + (1,) * (values.ndim - 1))
        stay = jnp.where(keep, values, jnp.zeros_like(values))
        return jnp.concatenate([stay, from_prev[None], from_next[None]], axis=0)

    attn_prev = passed_along(picked(1, attn), "grp", 1)
    attn_next = passed_along(picked(2, attn), "grp", -1)

    cores = 2
    chips = devices // cores
    alike = [[cores * i + j for i in range(chips)] for j in range(cores)]
    pairs = [[cores * i + j for j in range(cores)] for i in range(chips)]
    count = chips * requests
    outgoing = jnp.broadcast_to(rows[None], (chips, requests, width))
    received = lax.all_to_all(
        outgoing, "ep", split_axis=0, concat_axis=0, axis_index_groups=alike, tiled=True
    )
    received, attn_prev, attn_next = lax.optimization_barrier((received, attn_prev, attn_next))
    x = lax.all_gather(
        received.reshape(count, width), "ep", axis_index_groups=pairs, axis=0, tiled=True
    )
    core = (lax.axis_index("ep") % cores).astype(jnp.int32).reshape(1)
    w_down = down_weight[0]
    act, part = pl.pallas_call(
        experts_kernel,
        out_shape=(
            jax.ShapeDtypeStruct((cores * count, w_down.shape[0]), jnp.bfloat16),
            jax.ShapeDtypeStruct((count, width), jnp.bfloat16),
        ),
        in_specs=in_vmem(5),
        out_specs=tuple(in_vmem(2)[1:]),
        compiler_params=LIMIT,
    )(core, x, norm_gain[None, :], gate_weight[0], up_weight[0], w_down)
    parts = lax.all_gather(part, "ep", axis_index_groups=pairs, axis=0, tiled=True)
    pair = pl.pallas_call(
        join_kernel,
        out_shape=jax.ShapeDtypeStruct((count, width), jnp.bfloat16),
        in_specs=in_vmem(3),
        out_specs=in_vmem(1)[1],
        compiler_params=LIMIT,
    )(core, act, parts, w_down)
    returned = lax.all_to_all(
        pair.reshape(chips, requests, width),
        "ep",
        split_axis=0,
        concat_axis=0,
        axis_index_groups=alike,
        tiled=True,
    )

    ids, gates, _ = lax.optimization_barrier((expert_ids[0, 0], expert_gates[0, 0], pair))
    onehot = (
        ids[:, :, None] == jnp.arange(experts_here, dtype=jnp.int32)
    ).astype(jnp.float32)
    mix = jnp.einsum("sk,skx->sx", gates, onehot, precision=lax.Precision.HIGHEST)
    mix_next = passed_along(mix[requests : requests + 1], "grp", -1)
    mix_prev = passed_along(mix[requests + 1 : requests + 2], "grp", 1)
    at = moves[:, None]
    mix_home = jnp.where(
        at == 0, mix[:requests], jnp.where(at == 1, mix_next, mix_prev)
    )

    per_expert = jnp.sum(
        returned.reshape(experts_here, SLICES // cores, requests, width).astype(jnp.float32), axis=1
    )
    moe = jnp.sum(per_expert * mix_home.T[:, :, None], axis=0).astype(jnp.bfloat16)
    moe_prev = passed_along(picked(1, moe), "grp", 1)
    moe_next = passed_along(picked(2, moe), "grp", -1)
    return (
        served(attn, attn_prev, attn_next)[None, None],
        served(moe, moe_prev, moe_next)[None, None],
    )


def solution(mesh):
    in_specs = (
        P("grp", "ep", None, None, None),
        P("grp", "ep", None, None),
        P("grp", "ep", None),
        P("grp", "ep", None),
        P("grp", "ep", None, None, None),
        P("grp", "ep", None, None),
        P(),
        P("grp", "ep", None, None),
        P("grp", "ep", None, None),
        P("ep", None, None),
        P("ep", None, None),
        P("ep", None, None),
    )
    out_specs = (P("grp", "ep", None, None, None), P("grp", "ep", None, None))
    return jax.shard_map(body, mesh=mesh, in_specs=in_specs, out_specs=out_specs, check_vma=False)
```

```python
import jax
import jax.numpy as jnp
from jax import lax
from jax.experimental import pallas as pl
from jax.experimental.pallas import tpu as pltpu
from jax.sharding import PartitionSpec as P

VDIM = 512
QK_DIM = 192
SLICES = 8


def attend_rows(questions, keys, lens):
    scores = jnp.einsum(
        "rhl,rtl->rht", questions, keys, preferred_element_type=jnp.float32
    ) * QK_DIM ** (-0.5)
    live = jnp.arange(keys.shape[1], dtype=jnp.int32)[None, None, :] < lens[:, None, None]
    scores = jnp.where(live, scores, jnp.float32(-1e30))
    top = jnp.max(scores, axis=2, keepdims=True)
    expo = jnp.exp(scores - top)
    probs = (expo / jnp.sum(expo, axis=2, keepdims=True)).astype(jnp.bfloat16)
    out = jnp.einsum("rht,rtv->rhv", probs, keys[:, :, :VDIM], preferred_element_type=jnp.float32)
    return out.astype(jnp.bfloat16)


def dot(left, right):
    return jnp.dot(left, right, preferred_element_type=jnp.float32)


def spread_kernel(rows, out):
    out[...] = jnp.broadcast_to(rows[...][None], out.shape)


def experts_kernel(x, gain, gate_a, up_a, down_a, gate_b, up_b, down_b, out):
    wide = x[...].astype(jnp.float32)
    scale = lax.rsqrt(jnp.mean(wide * wide, axis=1, keepdims=True) + 1e-06)
    normed = (wide * scale * gain[...]).astype(jnp.bfloat16)
    total = 0.0
    for gate, up, down in ((gate_a, up_a, down_a), (gate_b, up_b, down_b)):
        act = (jax.nn.silu(dot(normed, gate[...])) * dot(normed, up[...])).astype(jnp.bfloat16)
        total = total + dot(act, down[...])
    out[...] = total.astype(jnp.bfloat16).reshape(out.shape)


def in_vmem(count):
    return [pl.BlockSpec(memory_space=pltpu.VMEM) for _ in range(count)]


LIMIT = pltpu.CompilerParams(vmem_limit_bytes=16 * 1024 * 1024)


def body(
    latent_cache,
    page_table,
    lengths,
    move_to,
    query,
    hidden,
    norm_gain,
    expert_ids,
    expert_gates,
    gate_weight,
    up_weight,
    down_weight,
):
    pool = latent_cache[0, 0]
    table = page_table[0, 0]
    requests = table.shape[0]
    moves = move_to[0, 0]
    rows = hidden[0, 0]
    width = rows.shape[1]
    devices = lax.axis_size("ep")
    experts_here = devices // SLICES

    keys = pool[table.reshape(-1)].reshape(requests, table.shape[1] * pool.shape[1], pool.shape[2])
    attn = attend_rows(query[0, 0], keys, lengths[0, 0])

    def picked(which, values):
        keep = (moves == which).reshape((requests,) + (1,) * (values.ndim - 1))
        return jnp.sum(jnp.where(keep, values, jnp.zeros_like(values)), axis=0, dtype=values.dtype)

    def served(values, from_prev, from_next):
        keep = (moves == 0).reshape((requests,) + (1,) * (values.ndim - 1))
        stay = jnp.where(keep, values, jnp.zeros_like(values))
        return jnp.concatenate([stay, from_prev[None], from_next[None]], axis=0)

    def exchanged(forward, backward):
        groups = lax.axis_size("grp")
        even = lax.axis_index("grp") % 2 == 0
        outer = [(i, (i + 1) % groups if i % 2 else (i - 1) % groups) for i in range(groups)]
        inner = [(i, i ^ 1) for i in range(groups)]
        one = lax.ppermute(jnp.where(even, backward, forward), "grp", outer)
        two = lax.ppermute(jnp.where(even, forward, backward), "grp", inner)
        return jnp.where(even, one, two), jnp.where(even, two, one)

    cores = 2
    chips = devices // cores
    alike = [[cores * i + j for i in range(chips)] for j in range(cores)]
    count = chips * requests
    outgoing = pl.pallas_call(
        spread_kernel,
        out_shape=jax.ShapeDtypeStruct((chips, requests, width), jnp.bfloat16),
        in_specs=in_vmem(1),
        out_specs=in_vmem(1)[0],
    )(rows)
    received = lax.all_to_all(
        outgoing, "ep", split_axis=0, concat_axis=0, axis_index_groups=alike, tiled=True
    )
    swap = [(i, i ^ 1) for i in range(devices)]
    weights = (gate_weight[0], up_weight[0], down_weight[0])
    traded = tuple(lax.ppermute(weight, "ep", swap) for weight in weights)
    received, attn = lax.optimization_barrier((received, attn))
    pair = pl.pallas_call(
        experts_kernel,
        out_shape=jax.ShapeDtypeStruct((chips, requests, width), jnp.bfloat16),
        in_specs=in_vmem(8),
        out_specs=in_vmem(1)[0],
        compiler_params=LIMIT,
    )(received.reshape(count, width), norm_gain[None, :], *weights, *traded)
    returned = lax.all_to_all(
        pair,
        "ep",
        split_axis=0,
        concat_axis=0,
        axis_index_groups=alike,
        tiled=True,
    )

    ids, gates, attn, _ = lax.optimization_barrier((expert_ids[0, 0], expert_gates[0, 0], attn, pair))
    onehot = (
        ids[:, :, None] == jnp.arange(experts_here, dtype=jnp.int32)
    ).astype(jnp.float32)
    mix = jnp.einsum("sk,skx->sx", gates, onehot, precision=lax.Precision.HIGHEST)
    high = lax.reduce_precision(mix, 8, 7)
    middle = lax.reduce_precision(mix - high, 8, 7)
    low = lax.reduce_precision(mix - high - middle, 8, 7)
    pieces = jnp.concatenate([high, middle, low], axis=1).astype(jnp.bfloat16)
    pieces = jnp.pad(pieces, ((0, 0), (0, VDIM - pieces.shape[1])))[:, None, :]
    heads = attn.shape[1]
    behind = lambda row, values: jnp.concatenate([values, row], axis=0)
    got_prev, got_next = exchanged(
        behind(pieces[requests + 1], picked(1, attn)), behind(pieces[requests], picked(2, attn))
    )
    per_expert = jnp.sum(
        returned.reshape(experts_here, SLICES // cores, requests, width).astype(jnp.float32), axis=1
    )
    per_expert, got_prev, got_next = lax.optimization_barrier((per_expert, got_prev, got_next))
    attn_prev, attn_next = got_prev[:heads], got_next[:heads]

    def mix_of(got):
        three = got[heads, : 3 * experts_here].astype(jnp.float32).reshape(3, experts_here)
        return (three[0] + three[1] + three[2])[None]

    at = moves[:, None]
    mix_home = jnp.where(
        at == 0, mix[:requests], jnp.where(at == 1, mix_of(got_next), mix_of(got_prev))
    )
    moe = jnp.sum(per_expert * mix_home.T[:, :, None], axis=0).astype(jnp.bfloat16)
    moe_prev, moe_next = exchanged(picked(1, moe), picked(2, moe))
    return (
        served(attn, attn_prev, attn_next)[None, None],
        served(moe, moe_prev, moe_next)[None, None],
    )


def solution(mesh):
    in_specs = (
        P("grp", "ep", None, None, None),
        P("grp", "ep", None, None),
        P("grp", "ep", None),
        P("grp", "ep", None),
        P("grp", "ep", None, None, None),
        P("grp", "ep", None, None),
        P(),
        P("grp", "ep", None, None),
        P("grp", "ep", None, None),
        P("ep", None, None),
        P("ep", None, None),
        P("ep", None, None),
    )
    out_specs = (P("grp", "ep", None, None, None), P("grp", "ep", None, None))
    return jax.shard_map(body, mesh=mesh, in_specs=in_specs, out_specs=out_specs, check_vma=False)
```

```python
import functools

import jax
import jax.numpy as jnp
from jax import lax
from jax.experimental import pallas as pl
from jax.experimental.pallas import tpu as pltpu
from jax.sharding import PartitionSpec as P

VDIM = 512
QK_DIM = 192
SLICES = 8
BEHIND = 16


def dot(left, right):
    return jnp.dot(left, right, preferred_element_type=jnp.float32)


def one_of(choices, which, wanted):
    found = jnp.zeros_like(choices[0])
    for j, choice in enumerate(choices):
        found = jnp.where(which[j] == wanted, choice, found)
    return found


def spread_kernel(rows, out):
    out[...] = jnp.broadcast_to(rows[...][None], out.shape)


def attend_kernel(
    table, lens, moves, odd, ids, gates, pool, query, outer, inner, stay, mix
):
    requests, heads = query.shape[0], query.shape[1]
    results = []
    for j in range(requests):
        keys = jnp.concatenate([pool[table[j, p]] for p in range(table.shape[1])], axis=0)
        scores = lax.dot_general(
            query[j], keys, (((1,), (1,)), ((), ())), preferred_element_type=jnp.float32
        ) * QK_DIM ** (-0.5)
        live = lax.broadcasted_iota(jnp.int32, scores.shape, 1) < lens[j]
        scores = jnp.where(live, scores, jnp.float32(-1e30))
        expo = jnp.exp(scores - jnp.max(scores, axis=1, keepdims=True))
        probs = (expo / jnp.sum(expo, axis=1, keepdims=True)).astype(jnp.bfloat16)
        results.append(dot(probs, keys[:, :VDIM]))
        stay[j] = jnp.where(moves[j] == 0, results[j], jnp.zeros_like(results[j])).astype(jnp.bfloat16)
    lane = lax.broadcasted_iota(jnp.int32, mix.shape, 1)
    total = jnp.zeros(mix.shape, jnp.float32)
    for k in range(ids.shape[1]):
        total = total + jnp.where(ids[:, k : k + 1] == lane, gates[:, k : k + 1], 0.0)
    mix[...] = total
    high = total.astype(jnp.bfloat16).astype(jnp.float32)
    middle = (total - high).astype(jnp.bfloat16).astype(jnp.float32)
    low = total - high - middle
    pieces = jnp.concatenate([high, middle, low, jnp.zeros_like(low)], axis=1)
    forward, backward = one_of(results, moves, 1), one_of(results, moves, 2)
    behind = outer.shape[0] - heads
    row_forward = jnp.broadcast_to(pieces[requests + 1 : requests + 2], (behind, pieces.shape[1]))
    row_backward = jnp.broadcast_to(pieces[requests : requests + 1], (behind, pieces.shape[1]))
    is_odd = odd[0] == 1
    outer[:heads] = jnp.where(is_odd, forward, backward).astype(jnp.bfloat16)
    outer[heads:] = jnp.where(is_odd, row_forward, row_backward).astype(jnp.bfloat16)
    inner[:heads] = jnp.where(is_odd, backward, forward).astype(jnp.bfloat16)
    inner[heads:] = jnp.where(is_odd, row_backward, row_forward).astype(jnp.bfloat16)


def experts_kernel(
    x, gain, gate_a, up_a, down_a, gate_there, up_there, down_there, out, gate_b, up_b, down_b, sems
):
    pairs = ((gate_there, gate_b), (up_there, up_b), (down_there, down_b))
    copies = [pltpu.make_async_copy(*pair, sems.at[i]) for i, pair in enumerate(pairs)]
    for copy in copies:
        copy.start()
    wide = x[...].reshape(x.shape[0] * x.shape[1], x.shape[2]).astype(jnp.float32)
    scale = lax.rsqrt(jnp.mean(wide * wide, axis=1, keepdims=True) + 1e-06)
    normed = (wide * scale * gain[...]).astype(jnp.bfloat16)
    act = (jax.nn.silu(dot(normed, gate_a[...])) * dot(normed, up_a[...])).astype(jnp.bfloat16)
    total = dot(act, down_a[...])
    copies[0].wait()
    gate = dot(normed, gate_b[...])
    copies[1].wait()
    act = (jax.nn.silu(gate) * dot(normed, up_b[...])).astype(jnp.bfloat16)
    copies[2].wait()
    total = total + dot(act, down_b[...])
    out[...] = total.astype(jnp.bfloat16).reshape(out.shape)


def gather_kernel(experts_here, moves, odd, returned, mix, got_outer, got_inner, outer, inner, stay):
    chips, requests, width = returned.shape
    experts = experts_here
    is_odd = odd[0] == 1
    heads = got_outer.shape[0] - BEHIND

    def mix_of(got):
        row = got[heads : heads + BEHIND].astype(jnp.float32)[:1]
        step = mix.shape[1]
        return row[:, :step] + row[:, step : 2 * step] + row[:, 2 * step : 3 * step]

    mix_outer, mix_inner = mix_of(got_outer), mix_of(got_inner)
    mix_next = jnp.where(is_odd, mix_outer, mix_inner)
    mix_prev = jnp.where(is_odd, mix_inner, mix_outer)
    lane = lax.broadcasted_iota(jnp.int32, (1, chips * requests), 1)
    weights = []
    for j in range(requests):
        own = mix[j : j + 1]
        home = jnp.where(moves[j] == 0, own, jnp.where(moves[j] == 1, mix_next, mix_prev))
        spread = jnp.zeros(lane.shape, jnp.float32)
        per_expert = chips * requests // experts
        for x in range(experts):
            spread = jnp.where(lane // per_expert == x, home[:, x : x + 1], spread)
        weights.append(jnp.where(lane % requests == j, spread, 0.0))
    weights = jnp.concatenate(weights, axis=0)
    flat = returned[...].reshape(chips * requests, width)
    high = weights.astype(jnp.bfloat16)
    rest = weights - high.astype(jnp.float32)
    middle = rest.astype(jnp.bfloat16)
    low = (rest - middle.astype(jnp.float32)).astype(jnp.bfloat16)
    moe = dot(high, flat) + dot(middle, flat) + dot(low, flat)
    rows = [moe[j : j + 1] for j in range(requests)]
    forward, backward = one_of(rows, moves, 1), one_of(rows, moves, 2)
    outer[...] = jnp.where(is_odd, forward, backward).astype(jnp.bfloat16)
    inner[...] = jnp.where(is_odd, backward, forward).astype(jnp.bfloat16)
    kept = [jnp.where(moves[j] == 0, rows[j], jnp.zeros_like(rows[j])) for j in range(requests)]
    stay[...] = jnp.concatenate(kept, axis=0).astype(jnp.bfloat16)


def in_vmem(count):
    return [pl.BlockSpec(memory_space=pltpu.VMEM) for _ in range(count)]


def in_smem(count):
    return [pl.BlockSpec(memory_space=pltpu.SMEM) for _ in range(count)]


SMALL = pltpu.CompilerParams(vmem_limit_bytes=6 * 1024 * 1024)
LIMIT = pltpu.CompilerParams(vmem_limit_bytes=10 * 1024 * 1024)


def body(
    latent_cache,
    page_table,
    lengths,
    move_to,
    query,
    hidden,
    norm_gain,
    expert_ids,
    expert_gates,
    gate_weight,
    up_weight,
    down_weight,
):
    pool = latent_cache[0, 0]
    table = page_table[0, 0]
    requests = table.shape[0]
    moves = move_to[0, 0]
    rows = hidden[0, 0]
    width = rows.shape[1]
    devices = lax.axis_size("ep")

    groups = lax.axis_size("grp")
    group_odd = (lax.axis_index("grp") % 2).astype(jnp.int32).reshape(1)
    outer_pairs = [(i, (i + 1) % groups if i % 2 else (i - 1) % groups) for i in range(groups)]
    inner_pairs = [(i, i ^ 1) for i in range(groups)]

    def exchanged(outer, inner):
        return lax.ppermute(outer, "grp", outer_pairs), lax.ppermute(inner, "grp", inner_pairs)

    def served(stay, got_outer, got_inner):
        odd = group_odd[0] == 1
        from_prev = jnp.where(odd, got_inner, got_outer)
        from_next = jnp.where(odd, got_outer, got_inner)
        return jnp.concatenate([stay, from_prev, from_next], axis=0)[None, None]

    heads = query.shape[3]
    payload = jax.ShapeDtypeStruct((heads + BEHIND, VDIM), jnp.bfloat16)
    send_outer, send_inner, attn_stay, mix = pl.pallas_call(
        attend_kernel,
        out_shape=(
            payload,
            payload,
            jax.ShapeDtypeStruct((requests, heads, VDIM), jnp.bfloat16),
            jax.ShapeDtypeStruct((expert_ids.shape[2], 128), jnp.float32),
        ),
        in_specs=in_smem(4) + in_vmem(4),
        out_specs=tuple(in_vmem(4)),
        compiler_params=SMALL,
        cost_estimate=pl.CostEstimate(flops=40_000_000_000, bytes_accessed=400_000_000, transcendentals=100_000_000),
    )(
        table, lengths[0, 0], moves, group_odd, expert_ids[0, 0], expert_gates[0, 0], pool, query[0, 0]
    )

    cores = 2
    chips = devices // cores
    alike = [[cores * i + j for i in range(chips)] for j in range(cores)]
    count = chips * requests
    outgoing = pl.pallas_call(
        spread_kernel,
        out_shape=jax.ShapeDtypeStruct((chips, requests, width), jnp.bfloat16),
        in_specs=in_vmem(1),
        out_specs=in_vmem(1)[0],
        compiler_params=pltpu.CompilerParams(vmem_limit_bytes=2 * 1024 * 1024),
    )(rows)
    received = lax.all_to_all(
        outgoing, "ep", split_axis=0, concat_axis=0, axis_index_groups=alike, tiled=True
    )
    swap = [(i, i ^ 1) for i in range(devices)]
    weights = (gate_weight[0], up_weight[0], down_weight[0])
    traded = tuple(lax.ppermute(weight, "ep", swap) for weight in weights)
    received, send_outer, send_inner, attn_stay, mix = lax.optimization_barrier(
        (received, send_outer, send_inner, attn_stay, mix)
    )
    pair = pl.pallas_call(
        experts_kernel,
        out_shape=jax.ShapeDtypeStruct((chips, requests, width), jnp.bfloat16),
        in_specs=in_vmem(5) + [pl.BlockSpec(memory_space=pl.ANY) for _ in traded],
        out_specs=in_vmem(1)[0],
        scratch_shapes=[pltpu.VMEM(weight.shape, weight.dtype) for weight in traded]
        + [pltpu.SemaphoreType.DMA((len(traded),))],
        compiler_params=LIMIT,
    )(received, norm_gain[None, :], *weights, *traded)
    returned = lax.all_to_all(
        pair,
        "ep",
        split_axis=0,
        concat_axis=0,
        axis_index_groups=alike,
        tiled=True,
    )

    send_outer, send_inner, attn_stay, _ = lax.optimization_barrier(
        (send_outer, send_inner, attn_stay, pair)
    )
    got_outer, got_inner = exchanged(send_outer, send_inner)
    returned, got_outer, got_inner = lax.optimization_barrier((returned, got_outer, got_inner))
    line = jax.ShapeDtypeStruct((1, width), jnp.bfloat16)
    moe_outer, moe_inner, moe_stay = pl.pallas_call(
        functools.partial(gather_kernel, devices // SLICES),
        out_shape=(line, line, jax.ShapeDtypeStruct((requests, width), jnp.bfloat16)),
        in_specs=in_smem(2) + in_vmem(4),
        out_specs=tuple(in_vmem(3)),
        compiler_params=SMALL,
    )(moves, group_odd, returned, mix, got_outer, got_inner)
    return (
        served(attn_stay, got_outer[None, :heads], got_inner[None, :heads]),
        served(moe_stay, *exchanged(moe_outer, moe_inner)),
    )


def solution(mesh):
    in_specs = (
        P("grp", "ep", None, None, None),
        P("grp", "ep", None, None),
        P("grp", "ep", None),
        P("grp", "ep", None),
        P("grp", "ep", None, None, None),
        P("grp", "ep", None, None),
        P(),
        P("grp", "ep", None, None),
        P("grp", "ep", None, None),
        P("ep", None, None),
        P("ep", None, None),
        P("ep", None, None),
    )
    out_specs = (P("grp", "ep", None, None, None), P("grp", "ep", None, None))
    return jax.shard_map(body, mesh=mesh, in_specs=in_specs, out_specs=out_specs, check_vma=False)
```

```python
import functools

import jax
import jax.numpy as jnp
from jax import lax
from jax.experimental import pallas as pl
from jax.experimental.pallas import tpu as pltpu
from jax.sharding import PartitionSpec as P

VDIM = 512
QK_DIM = 192
SLICES = 8
BEHIND = 16


def dot(left, right):
    return jnp.dot(left, right, preferred_element_type=jnp.float32)


def one_of(choices, which, wanted):
    found = jnp.zeros_like(choices[0])
    for j, choice in enumerate(choices):
        found = jnp.where(which[j] == wanted, choice, found)
    return found


def spread_kernel(rows, out):
    out[...] = jnp.broadcast_to(rows[...][None], out.shape)


def attend_kernel(
    table, lens, moves, odd, ids, gates, pool, query, outer, inner, stay, mix
):
    requests, heads = query.shape[0], query.shape[1]
    results = []
    for j in range(requests):
        keys = jnp.concatenate([pool[table[j, p]] for p in range(table.shape[1])], axis=0)
        scores = lax.dot_general(
            query[j], keys, (((1,), (1,)), ((), ())), preferred_element_type=jnp.float32
        ) * QK_DIM ** (-0.5)
        live = lax.broadcasted_iota(jnp.int32, scores.shape, 1) < lens[j]
        scores = jnp.where(live, scores, jnp.float32(-1e30))
        expo = jnp.exp(scores - jnp.max(scores, axis=1, keepdims=True))
        probs = (expo / jnp.sum(expo, axis=1, keepdims=True)).astype(jnp.bfloat16)
        results.append(dot(probs, keys[:, :VDIM]))
        stay[j] = jnp.where(moves[j] == 0, results[j], jnp.zeros_like(results[j])).astype(jnp.bfloat16)
    rows = ids.shape[0]
    lane = lax.broadcasted_iota(jnp.int32, (rows, mix.shape[1]), 1)
    total = jnp.zeros(lane.shape, jnp.float32)
    for k in range(ids.shape[1]):
        total = total + jnp.where(ids[:, k : k + 1] == lane, gates[:, k : k + 1], 0.0)
    mix[:rows] = total
    flags = [moves[j] for j in range(requests)] + [odd[0]]
    place = lax.broadcasted_iota(jnp.int32, (mix.shape[0] - rows, mix.shape[1]), 0)
    kept = jnp.zeros(place.shape, jnp.int32)
    for j, flag in enumerate(flags):
        kept = jnp.where(place == j, flag, kept)
    mix[rows:] = kept.astype(jnp.float32)
    high = total.astype(jnp.bfloat16).astype(jnp.float32)
    middle = (total - high).astype(jnp.bfloat16).astype(jnp.float32)
    low = total - high - middle
    pieces = jnp.concatenate([high, middle, low, jnp.zeros_like(low)], axis=1)
    forward, backward = one_of(results, moves, 1), one_of(results, moves, 2)
    behind = outer.shape[0] - heads
    row_forward = jnp.broadcast_to(pieces[requests + 1 : requests + 2], (behind, pieces.shape[1]))
    row_backward = jnp.broadcast_to(pieces[requests : requests + 1], (behind, pieces.shape[1]))
    is_odd = odd[0] == 1
    outer[:heads] = jnp.where(is_odd, forward, backward).astype(jnp.bfloat16)
    outer[heads:] = jnp.where(is_odd, row_forward, row_backward).astype(jnp.bfloat16)
    inner[:heads] = jnp.where(is_odd, backward, forward).astype(jnp.bfloat16)
    inner[heads:] = jnp.where(is_odd, row_backward, row_forward).astype(jnp.bfloat16)


def experts_kernel(
    x, gain, gate_a, up_a, down_a, gate_there, up_there, down_there, out, gate_b, up_b, down_b, sems
):
    pairs = ((gate_there, gate_b), (up_there, up_b), (down_there, down_b))
    copies = [pltpu.make_async_copy(*pair, sems.at[i]) for i, pair in enumerate(pairs)]
    for copy in copies:
        copy.start()
    wide = x[...].reshape(x.shape[0] * x.shape[1], x.shape[2]).astype(jnp.float32)
    scale = lax.rsqrt(jnp.mean(wide * wide, axis=1, keepdims=True) + 1e-06)
    normed = (wide * scale * gain[...]).astype(jnp.bfloat16)
    act = (jax.nn.silu(dot(normed, gate_a[...])) * dot(normed, up_a[...])).astype(jnp.bfloat16)
    total = dot(act, down_a[...])
    copies[0].wait()
    gate = dot(normed, gate_b[...])
    copies[1].wait()
    act = (jax.nn.silu(gate) * dot(normed, up_b[...])).astype(jnp.bfloat16)
    copies[2].wait()
    total = total + dot(act, down_b[...])
    out[...] = total.astype(jnp.bfloat16).reshape(out.shape)


def gather_kernel(experts, returned, mix, got_outer, got_inner, outer, inner, stay):
    chips, requests, width = returned.shape
    rows_served = mix.shape[0] - requests - 2
    moves = [mix[rows_served + j : rows_served + j + 1] for j in range(requests)]
    odd = mix[rows_served + requests : rows_served + requests + 1]
    is_odd = odd == 1.0
    heads = got_outer.shape[0] - BEHIND

    def mix_of(got):
        row = got[heads : heads + BEHIND].astype(jnp.float32)[:1]
        step = mix.shape[1]
        return row[:, :step] + row[:, step : 2 * step] + row[:, 2 * step : 3 * step]

    mix_outer, mix_inner = mix_of(got_outer), mix_of(got_inner)
    mix_next = jnp.where(is_odd, mix_outer, mix_inner)
    mix_prev = jnp.where(is_odd, mix_inner, mix_outer)
    lane = lax.broadcasted_iota(jnp.int32, (1, chips * requests), 1)
    weights = []
    for j in range(requests):
        own = mix[j : j + 1]
        home = jnp.where(moves[j] == 0, own, jnp.where(moves[j] == 1, mix_next, mix_prev))
        spread = jnp.zeros(lane.shape, jnp.float32)
        per_expert = chips * requests // experts
        for x in range(experts):
            spread = jnp.where(lane // per_expert == x, home[:, x : x + 1], spread)
        weights.append(jnp.where(lane % requests == j, spread, 0.0))
    weights = jnp.concatenate(weights, axis=0)
    flat = returned[...].reshape(chips * requests, width)
    high = weights.astype(jnp.bfloat16)
    rest = weights - high.astype(jnp.float32)
    middle = rest.astype(jnp.bfloat16)
    low = (rest - middle.astype(jnp.float32)).astype(jnp.bfloat16)
    moe = dot(high, flat) + dot(middle, flat) + dot(low, flat)
    rows = [moe[j : j + 1] for j in range(requests)]
    moves = [jnp.broadcast_to(move[:, :1], (1, width)) for move in moves]
    is_odd = jnp.broadcast_to(odd[:, :1], (1, width)) == 1.0
    forward, backward = one_of(rows, moves, 1), one_of(rows, moves, 2)
    outer[...] = jnp.where(is_odd, forward, backward).astype(jnp.bfloat16)
    inner[...] = jnp.where(is_odd, backward, forward).astype(jnp.bfloat16)
    kept = [jnp.where(moves[j] == 0, rows[j], jnp.zeros_like(rows[j])) for j in range(requests)]
    stay[...] = jnp.concatenate(kept, axis=0).astype(jnp.bfloat16)


def in_vmem(count):
    return [pl.BlockSpec(memory_space=pltpu.VMEM) for _ in range(count)]


def in_smem(count):
    return [pl.BlockSpec(memory_space=pltpu.SMEM) for _ in range(count)]


SMALL = pltpu.CompilerParams(vmem_limit_bytes=6 * 1024 * 1024)
LIMIT = pltpu.CompilerParams(vmem_limit_bytes=10 * 1024 * 1024)


def body(
    latent_cache,
    page_table,
    lengths,
    move_to,
    query,
    hidden,
    norm_gain,
    expert_ids,
    expert_gates,
    gate_weight,
    up_weight,
    down_weight,
):
    pool = latent_cache[0, 0]
    table = page_table[0, 0]
    requests = table.shape[0]
    moves = move_to[0, 0]
    rows = hidden[0, 0]
    width = rows.shape[1]
    devices = lax.axis_size("ep")

    groups = lax.axis_size("grp")
    group_odd = (lax.axis_index("grp") % 2).astype(jnp.int32).reshape(1)
    outer_pairs = [(i, (i + 1) % groups if i % 2 else (i - 1) % groups) for i in range(groups)]
    inner_pairs = [(i, i ^ 1) for i in range(groups)]

    def exchanged(outer, inner):
        return lax.ppermute(outer, "grp", outer_pairs), lax.ppermute(inner, "grp", inner_pairs)

    def served(stay, got_outer, got_inner):
        odd = group_odd[0] == 1
        from_prev = jnp.where(odd, got_inner, got_outer)
        from_next = jnp.where(odd, got_outer, got_inner)
        return jnp.concatenate([stay, from_prev, from_next], axis=0)[None, None]

    heads = query.shape[3]
    payload = jax.ShapeDtypeStruct((heads + BEHIND, VDIM), jnp.bfloat16)
    send_outer, send_inner, attn_stay, mix = pl.pallas_call(
        attend_kernel,
        out_shape=(
            payload,
            payload,
            jax.ShapeDtypeStruct((requests, heads, VDIM), jnp.bfloat16),
            jax.ShapeDtypeStruct((expert_ids.shape[2] + requests + 2, 128), jnp.float32),
        ),
        in_specs=in_smem(4) + in_vmem(4),
        out_specs=tuple(in_vmem(4)),
        compiler_params=SMALL,
        cost_estimate=pl.CostEstimate(flops=40_000_000_000, bytes_accessed=400_000_000, transcendentals=100_000_000),
    )(
        table, lengths[0, 0], moves, group_odd, expert_ids[0, 0], expert_gates[0, 0], pool, query[0, 0]
    )

    cores = 2
    chips = devices // cores
    alike = [[cores * i + j for i in range(chips)] for j in range(cores)]
    count = chips * requests
    outgoing = pl.pallas_call(
        spread_kernel,
        out_shape=jax.ShapeDtypeStruct((chips, requests, width), jnp.bfloat16),
        in_specs=in_vmem(1),
        out_specs=in_vmem(1)[0],
        compiler_params=pltpu.CompilerParams(vmem_limit_bytes=2 * 1024 * 1024),
    )(rows)
    received = lax.all_to_all(
        outgoing, "ep", split_axis=0, concat_axis=0, axis_index_groups=alike, tiled=True
    )
    swap = [(i, i ^ 1) for i in range(devices)]
    weights = (gate_weight[0], up_weight[0], down_weight[0])
    traded = tuple(lax.ppermute(weight, "ep", swap) for weight in weights)
    received, send_outer, send_inner, attn_stay, mix = lax.optimization_barrier(
        (received, send_outer, send_inner, attn_stay, mix)
    )
    pair = pl.pallas_call(
        experts_kernel,
        out_shape=jax.ShapeDtypeStruct((chips, requests, width), jnp.bfloat16),
        in_specs=in_vmem(5) + [pl.BlockSpec(memory_space=pl.ANY) for _ in traded],
        out_specs=in_vmem(1)[0],
        scratch_shapes=[pltpu.VMEM(weight.shape, weight.dtype) for weight in traded]
        + [pltpu.SemaphoreType.DMA((len(traded),))],
        compiler_params=LIMIT,
    )(received, norm_gain[None, :], *weights, *traded)
    returned = lax.all_to_all(
        pair,
        "ep",
        split_axis=0,
        concat_axis=0,
        axis_index_groups=alike,
        tiled=True,
    )

    send_outer, send_inner, attn_stay, _ = lax.optimization_barrier(
        (send_outer, send_inner, attn_stay, pair)
    )
    got_outer, got_inner = exchanged(send_outer, send_inner)
    returned, got_outer, got_inner = lax.optimization_barrier((returned, got_outer, got_inner))
    line = jax.ShapeDtypeStruct((1, width), jnp.bfloat16)
    moe_outer, moe_inner, moe_stay = pl.pallas_call(
        functools.partial(gather_kernel, devices // SLICES),
        out_shape=(line, line, jax.ShapeDtypeStruct((requests, width), jnp.bfloat16)),
        in_specs=in_vmem(4),
        out_specs=tuple(in_vmem(3)),
        compiler_params=SMALL,
    )(returned, mix, got_outer, got_inner)
    return (
        served(attn_stay, got_outer[None, :heads], got_inner[None, :heads]),
        served(moe_stay, *exchanged(moe_outer, moe_inner)),
    )


def solution(mesh):
    in_specs = (
        P("grp", "ep", None, None, None),
        P("grp", "ep", None, None),
        P("grp", "ep", None),
        P("grp", "ep", None),
        P("grp", "ep", None, None, None),
        P("grp", "ep", None, None),
        P(),
        P("grp", "ep", None, None),
        P("grp", "ep", None, None),
        P("ep", None, None),
        P("ep", None, None),
        P("ep", None, None),
    )
    out_specs = (P("grp", "ep", None, None, None), P("grp", "ep", None, None))
    return jax.shard_map(body, mesh=mesh, in_specs=in_specs, out_specs=out_specs, check_vma=False)
```

```python
import functools

import jax
import jax.numpy as jnp
from jax import lax
from jax.experimental import pallas as pl
from jax.experimental.pallas import tpu as pltpu
from jax.sharding import PartitionSpec as P

VDIM = 512
QK_DIM = 192
SLICES = 8
BEHIND = 16
PIECES = 2


def dot(left, right):
    return jnp.dot(left, right, preferred_element_type=jnp.float32)


def one_of(choices, which, wanted):
    found = jnp.zeros_like(choices[0])
    for j, choice in enumerate(choices):
        found = jnp.where(which[j] == wanted, choice, found)
    return found


def spread_kernel(rows, out):
    out[...] = jnp.broadcast_to(rows[...][None], out.shape)


def attend_kernel(
    table, lens, moves, odd, ids, gates, pool, query, outer, inner, stay, mix
):
    requests, heads = query.shape[0], query.shape[1]
    results = []
    for j in range(requests):
        keys = jnp.concatenate([pool[table[j, p]] for p in range(table.shape[1])], axis=0)
        scores = lax.dot_general(
            query[j], keys, (((1,), (1,)), ((), ())), preferred_element_type=jnp.float32
        ) * QK_DIM ** (-0.5)
        live = lax.broadcasted_iota(jnp.int32, scores.shape, 1) < lens[j]
        scores = jnp.where(live, scores, jnp.float32(-1e30))
        expo = jnp.exp(scores - jnp.max(scores, axis=1, keepdims=True))
        probs = (expo / jnp.sum(expo, axis=1, keepdims=True)).astype(jnp.bfloat16)
        results.append(dot(probs, keys[:, :VDIM]))
        stay[j] = jnp.where(moves[j] == 0, results[j], jnp.zeros_like(results[j])).astype(jnp.bfloat16)
    rows = ids.shape[0]
    lane = lax.broadcasted_iota(jnp.int32, (rows, mix.shape[1]), 1)
    total = jnp.zeros(lane.shape, jnp.float32)
    for k in range(ids.shape[1]):
        total = total + jnp.where(ids[:, k : k + 1] == lane, gates[:, k : k + 1], 0.0)
    mix[:rows] = total
    flags = [moves[j] for j in range(requests)] + [odd[0]]
    place = lax.broadcasted_iota(jnp.int32, (mix.shape[0] - rows, mix.shape[1]), 0)
    kept = jnp.zeros(place.shape, jnp.int32)
    for j, flag in enumerate(flags):
        kept = jnp.where(place == j, flag, kept)
    mix[rows:] = kept.astype(jnp.float32)
    high = total.astype(jnp.bfloat16).astype(jnp.float32)
    middle = (total - high).astype(jnp.bfloat16).astype(jnp.float32)
    low = total - high - middle
    pieces = jnp.concatenate([high, middle, low, jnp.zeros_like(low)], axis=1)
    forward, backward = one_of(results, moves, 1), one_of(results, moves, 2)
    behind = outer.shape[0] - heads
    row_forward = jnp.broadcast_to(pieces[requests + 1 : requests + 2], (behind, pieces.shape[1]))
    row_backward = jnp.broadcast_to(pieces[requests : requests + 1], (behind, pieces.shape[1]))
    is_odd = odd[0] == 1
    outer[:heads] = jnp.where(is_odd, forward, backward).astype(jnp.bfloat16)
    outer[heads:] = jnp.where(is_odd, row_forward, row_backward).astype(jnp.bfloat16)
    inner[:heads] = jnp.where(is_odd, backward, forward).astype(jnp.bfloat16)
    inner[heads:] = jnp.where(is_odd, row_backward, row_forward).astype(jnp.bfloat16)


def experts_kernel(
    x, gain, gate_a, up_a, down_a, gate_there, up_there, down_there, out, gate_b, up_b, down_b, pieces, sems, out_sems
):
    pairs = ((gate_there, gate_b), (up_there, up_b), (down_there, down_b))
    copies = [pltpu.make_async_copy(*pair, sems.at[i]) for i, pair in enumerate(pairs)]
    for copy in copies:
        copy.start()
    wide = x[...].reshape(x.shape[0] * x.shape[1], x.shape[2]).astype(jnp.float32)
    scale = lax.rsqrt(jnp.mean(wide * wide, axis=1, keepdims=True) + 1e-06)
    normed = (wide * scale * gain[...]).astype(jnp.bfloat16)
    act = (jax.nn.silu(dot(normed, gate_a[...])) * dot(normed, up_a[...])).astype(jnp.bfloat16)
    total = dot(act, down_a[...])
    copies[0].wait()
    gate = dot(normed, gate_b[...])
    copies[1].wait()
    act = (jax.nn.silu(gate) * dot(normed, up_b[...])).astype(jnp.bfloat16)
    copies[2].wait()
    leaving = []
    for i in range(PIECES):
        size = out.shape[2] // PIECES
        columns = slice(i * size, (i + 1) * size)
        piece = total[:, columns] + dot(act, down_b[:, columns])
        pieces[i] = piece.astype(jnp.bfloat16).reshape(pieces.shape[1:])
        leaving.append(pltpu.make_async_copy(pieces.at[i], out.at[:, :, columns], out_sems.at[i]))
        leaving[i].start()
    for copy in leaving:
        copy.wait()


def gather_kernel(experts, returned, mix, got_outer, got_inner, outer, inner, stay):
    chips, requests, width = returned.shape
    rows_served = mix.shape[0] - requests - 2
    moves = [mix[rows_served + j : rows_served + j + 1] for j in range(requests)]
    odd = mix[rows_served + requests : rows_served + requests + 1]
    is_odd = odd == 1.0
    heads = got_outer.shape[0] - BEHIND

    def mix_of(got):
        row = got[heads : heads + BEHIND].astype(jnp.float32)[:1]
        step = mix.shape[1]
        return row[:, :step] + row[:, step : 2 * step] + row[:, 2 * step : 3 * step]

    mix_outer, mix_inner = mix_of(got_outer), mix_of(got_inner)
    mix_next = jnp.where(is_odd, mix_outer, mix_inner)
    mix_prev = jnp.where(is_odd, mix_inner, mix_outer)
    lane = lax.broadcasted_iota(jnp.int32, (1, chips * requests), 1)
    weights = []
    for j in range(requests):
        own = mix[j : j + 1]
        home = jnp.where(moves[j] == 0, own, jnp.where(moves[j] == 1, mix_next, mix_prev))
        spread = jnp.zeros(lane.shape, jnp.float32)
        per_expert = chips * requests // experts
        for x in range(experts):
            spread = jnp.where(lane // per_expert == experts - 1 - x, home[:, x : x + 1], spread)
        weights.append(jnp.where(lane % requests == j, spread, 0.0))
    weights = jnp.concatenate(weights, axis=0)
    flat = returned[...].reshape(chips * requests, width)
    high = weights.astype(jnp.bfloat16)
    rest = weights - high.astype(jnp.float32)
    middle = rest.astype(jnp.bfloat16)
    low = (rest - middle.astype(jnp.float32)).astype(jnp.bfloat16)
    moe = dot(high, flat) + dot(middle, flat) + dot(low, flat)
    rows = [moe[j : j + 1] for j in range(requests)]
    moves = [jnp.broadcast_to(move[:, :1], (1, width)) for move in moves]
    is_odd = jnp.broadcast_to(odd[:, :1], (1, width)) == 1.0
    forward, backward = one_of(rows, moves, 1), one_of(rows, moves, 2)
    outer[...] = jnp.where(is_odd, forward, backward).astype(jnp.bfloat16)
    inner[...] = jnp.where(is_odd, backward, forward).astype(jnp.bfloat16)
    kept = [jnp.where(moves[j] == 0, rows[j], jnp.zeros_like(rows[j])) for j in range(requests)]
    stay[...] = jnp.concatenate(kept, axis=0).astype(jnp.bfloat16)


def in_vmem(count):
    return [pl.BlockSpec(memory_space=pltpu.VMEM) for _ in range(count)]


def in_smem(count):
    return [pl.BlockSpec(memory_space=pltpu.SMEM) for _ in range(count)]


SMALL = pltpu.CompilerParams(vmem_limit_bytes=6 * 1024 * 1024)
LIMIT = pltpu.CompilerParams(vmem_limit_bytes=10 * 1024 * 1024)


def body(
    latent_cache,
    page_table,
    lengths,
    move_to,
    query,
    hidden,
    norm_gain,
    expert_ids,
    expert_gates,
    gate_weight,
    up_weight,
    down_weight,
):
    pool = latent_cache[0, 0]
    table = page_table[0, 0]
    requests = table.shape[0]
    moves = move_to[0, 0]
    rows = hidden[0, 0]
    width = rows.shape[1]
    devices = lax.axis_size("ep")

    groups = lax.axis_size("grp")
    group_odd = (lax.axis_index("grp") % 2).astype(jnp.int32).reshape(1)
    outer_pairs = [(i, (i + 1) % groups if i % 2 else (i - 1) % groups) for i in range(groups)]
    inner_pairs = [(i, i ^ 1) for i in range(groups)]

    def exchanged(outer, inner):
        return lax.ppermute(outer, "grp", outer_pairs), lax.ppermute(inner, "grp", inner_pairs)

    def served(stay, got_outer, got_inner):
        odd = group_odd[0] == 1
        from_prev = jnp.where(odd, got_inner, got_outer)
        from_next = jnp.where(odd, got_outer, got_inner)
        return jnp.concatenate([stay, from_prev, from_next], axis=0)[None, None]

    heads = query.shape[3]
    payload = jax.ShapeDtypeStruct((heads + BEHIND, VDIM), jnp.bfloat16)
    send_outer, send_inner, attn_stay, mix = pl.pallas_call(
        attend_kernel,
        out_shape=(
            payload,
            payload,
            jax.ShapeDtypeStruct((requests, heads, VDIM), jnp.bfloat16),
            jax.ShapeDtypeStruct((expert_ids.shape[2] + requests + 2, 128), jnp.float32),
        ),
        in_specs=in_smem(4) + in_vmem(4),
        out_specs=tuple(in_vmem(4)),
        compiler_params=SMALL,
        cost_estimate=pl.CostEstimate(flops=40_000_000_000, bytes_accessed=400_000_000, transcendentals=100_000_000),
    )(
        table, lengths[0, 0], moves, group_odd, expert_ids[0, 0], expert_gates[0, 0], pool, query[0, 0]
    )

    cores = 2
    chips = devices // cores
    alike = [[cores * i + j for i in reversed(range(chips))] for j in range(cores)]
    count = chips * requests
    outgoing = pl.pallas_call(
        spread_kernel,
        out_shape=jax.ShapeDtypeStruct((chips, requests, width), jnp.bfloat16),
        in_specs=in_vmem(1),
        out_specs=in_vmem(1)[0],
        compiler_params=pltpu.CompilerParams(vmem_limit_bytes=2 * 1024 * 1024),
    )(rows)
    received = lax.all_to_all(
        outgoing, "ep", split_axis=0, concat_axis=0, axis_index_groups=alike, tiled=True
    )
    swap = [(i, i ^ 1) for i in range(devices)]
    weights = (gate_weight[0], up_weight[0], down_weight[0])
    traded = tuple(lax.ppermute(weight, "ep", swap) for weight in weights)
    received, send_outer, send_inner, attn_stay, mix = lax.optimization_barrier(
        (received, send_outer, send_inner, attn_stay, mix)
    )
    pair = pl.pallas_call(
        experts_kernel,
        out_shape=jax.ShapeDtypeStruct((chips, requests, width), jnp.bfloat16),
        in_specs=in_vmem(5) + [pl.BlockSpec(memory_space=pl.ANY) for _ in traded],
        out_specs=pl.BlockSpec(memory_space=pl.ANY),
        scratch_shapes=[pltpu.VMEM(weight.shape, weight.dtype) for weight in traded]
        + [pltpu.VMEM((PIECES, chips, requests, width // PIECES), jnp.bfloat16)]
        + [pltpu.SemaphoreType.DMA((len(traded),)), pltpu.SemaphoreType.DMA((PIECES,))],
        compiler_params=LIMIT,
    )(received, norm_gain[None, :], *weights, *traded)
    returned = lax.all_to_all(
        pair,
        "ep",
        split_axis=0,
        concat_axis=0,
        axis_index_groups=alike,
        tiled=True,
    )

    send_outer, send_inner, attn_stay, _ = lax.optimization_barrier(
        (send_outer, send_inner, attn_stay, pair)
    )
    got_outer, got_inner = exchanged(send_outer, send_inner)
    returned, got_outer, got_inner = lax.optimization_barrier((returned, got_outer, got_inner))
    line = jax.ShapeDtypeStruct((1, width), jnp.bfloat16)
    moe_outer, moe_inner, moe_stay = pl.pallas_call(
        functools.partial(gather_kernel, devices // SLICES),
        out_shape=(line, line, jax.ShapeDtypeStruct((requests, width), jnp.bfloat16)),
        in_specs=in_vmem(4),
        out_specs=tuple(in_vmem(3)),
        compiler_params=SMALL,
    )(returned, mix, got_outer, got_inner)
    return (
        served(attn_stay, got_outer[None, :heads], got_inner[None, :heads]),
        served(moe_stay, *exchanged(moe_outer, moe_inner)),
    )


def solution(mesh):
    in_specs = (
        P("grp", "ep", None, None, None),
        P("grp", "ep", None, None),
        P("grp", "ep", None),
        P("grp", "ep", None),
        P("grp", "ep", None, None, None),
        P("grp", "ep", None, None),
        P(),
        P("grp", "ep", None, None),
        P("grp", "ep", None, None),
        P("ep", None, None),
        P("ep", None, None),
        P("ep", None, None),
    )
    out_specs = (P("grp", "ep", None, None, None), P("grp", "ep", None, None))
    return jax.shard_map(body, mesh=mesh, in_specs=in_specs, out_specs=out_specs, check_vma=False)
```

```python
import functools

import jax
import jax.numpy as jnp
from jax import lax
from jax.experimental import pallas as pl
from jax.experimental.pallas import tpu as pltpu
from jax.sharding import PartitionSpec as P

VDIM = 512
QK_DIM = 192
SLICES = 8
BEHIND = 16
PIECES = 2


def dot(left, right):
    return jnp.dot(left, right, preferred_element_type=jnp.float32)


def one_of(choices, which, wanted):
    found = jnp.zeros_like(choices[0])
    for j, choice in enumerate(choices):
        found = jnp.where(which[j] == wanted, choice, found)
    return found


def spread_kernel(rows, out):
    out[...] = jnp.broadcast_to(rows[...][None], out.shape)


def attend_kernel(
    table, lens, moves, ids, gates, pool, query, outer, inner, stay, mix
):
    odd = lax.rem(lax.axis_index("grp"), 2)
    requests, heads = query.shape[0], query.shape[1]
    results = []
    for j in range(requests):
        keys = jnp.concatenate([pool[table[j, p]] for p in range(table.shape[1])], axis=0)
        scores = lax.dot_general(
            query[j], keys, (((1,), (1,)), ((), ())), preferred_element_type=jnp.float32
        ) * QK_DIM ** (-0.5)
        live = lax.broadcasted_iota(jnp.int32, scores.shape, 1) < lens[j]
        scores = jnp.where(live, scores, jnp.float32(-1e30))
        expo = jnp.exp(scores - jnp.max(scores, axis=1, keepdims=True))
        probs = (expo / jnp.sum(expo, axis=1, keepdims=True)).astype(jnp.bfloat16)
        results.append(dot(probs, keys[:, :VDIM]))
        stay[j] = jnp.where(moves[j] == 0, results[j], jnp.zeros_like(results[j])).astype(jnp.bfloat16)
    rows = ids.shape[0]
    lane = lax.broadcasted_iota(jnp.int32, (rows, mix.shape[1]), 1)
    total = jnp.zeros(lane.shape, jnp.float32)
    for k in range(ids.shape[1]):
        total = total + jnp.where(ids[:, k : k + 1] == lane, gates[:, k : k + 1], 0.0)
    mix[:rows] = total
    flags = [moves[j] for j in range(requests)] + [odd]
    place = lax.broadcasted_iota(jnp.int32, (mix.shape[0] - rows, mix.shape[1]), 0)
    kept = jnp.zeros(place.shape, jnp.int32)
    for j, flag in enumerate(flags):
        kept = jnp.where(place == j, flag, kept)
    mix[rows:] = kept.astype(jnp.float32)
    high = total.astype(jnp.bfloat16).astype(jnp.float32)
    middle = (total - high).astype(jnp.bfloat16).astype(jnp.float32)
    low = total - high - middle
    pieces = jnp.concatenate([high, middle, low, jnp.zeros_like(low)], axis=1)
    forward, backward = one_of(results, moves, 1), one_of(results, moves, 2)
    behind = outer.shape[0] - heads
    row_forward = jnp.broadcast_to(pieces[requests + 1 : requests + 2], (behind, pieces.shape[1]))
    row_backward = jnp.broadcast_to(pieces[requests : requests + 1], (behind, pieces.shape[1]))
    is_odd = odd == 1
    outer[:heads] = jnp.where(is_odd, forward, backward).astype(jnp.bfloat16)
    outer[heads:] = jnp.where(is_odd, row_forward, row_backward).astype(jnp.bfloat16)
    inner[:heads] = jnp.where(is_odd, backward, forward).astype(jnp.bfloat16)
    inner[heads:] = jnp.where(is_odd, row_backward, row_forward).astype(jnp.bfloat16)


def experts_kernel(
    x, gain, gate_a, up_a, down_a, gate_there, up_there, down_there, out, gate_b, up_b, down_b, pieces, sems, out_sems
):
    pairs = ((gate_there, gate_b), (up_there, up_b), (down_there, down_b))
    copies = [pltpu.make_async_copy(*pair, sems.at[i]) for i, pair in enumerate(pairs)]
    for copy in copies:
        copy.start()
    wide = x[...].reshape(x.shape[0] * x.shape[1], x.shape[2]).astype(jnp.float32)
    scale = lax.rsqrt(jnp.mean(wide * wide, axis=1, keepdims=True) + 1e-06)
    normed = (wide * scale * gain[...]).astype(jnp.bfloat16)
    act = (jax.nn.silu(dot(normed, gate_a[...])) * dot(normed, up_a[...])).astype(jnp.bfloat16)
    total = dot(act, down_a[...])
    copies[0].wait()
    gate = dot(normed, gate_b[...])
    copies[1].wait()
    act = (jax.nn.silu(gate) * dot(normed, up_b[...])).astype(jnp.bfloat16)
    copies[2].wait()
    leaving = []
    for i in range(PIECES):
        size = out.shape[2] // PIECES
        columns = slice(i * size, (i + 1) * size)
        piece = total[:, columns] + dot(act, down_b[:, columns])
        pieces[i] = piece.astype(jnp.bfloat16).reshape(pieces.shape[1:])
        leaving.append(pltpu.make_async_copy(pieces.at[i], out.at[:, :, columns], out_sems.at[i]))
        leaving[i].start()
    for copy in leaving:
        copy.wait()


def gather_kernel(experts, returned, mix, got_outer, got_inner, outer, inner, stay):
    chips, requests, width = returned.shape
    rows_served = mix.shape[0] - requests - 2
    moves = [mix[rows_served + j : rows_served + j + 1] for j in range(requests)]
    odd = mix[rows_served + requests : rows_served + requests + 1]
    is_odd = odd == 1.0
    heads = got_outer.shape[0] - BEHIND

    def mix_of(got):
        row = got[heads : heads + BEHIND].astype(jnp.float32)[:1]
        step = mix.shape[1]
        return row[:, :step] + row[:, step : 2 * step] + row[:, 2 * step : 3 * step]

    mix_outer, mix_inner = mix_of(got_outer), mix_of(got_inner)
    mix_next = jnp.where(is_odd, mix_outer, mix_inner)
    mix_prev = jnp.where(is_odd, mix_inner, mix_outer)
    lane = lax.broadcasted_iota(jnp.int32, (1, chips * requests), 1)
    weights = []
    for j in range(requests):
        own = mix[j : j + 1]
        home = jnp.where(moves[j] == 0, own, jnp.where(moves[j] == 1, mix_next, mix_prev))
        spread = jnp.zeros(lane.shape, jnp.float32)
        per_expert = chips * requests // experts
        for x in range(experts):
            spread = jnp.where(lane // per_expert == experts - 1 - x, home[:, x : x + 1], spread)
        weights.append(jnp.where(lane % requests == j, spread, 0.0))
    weights = jnp.concatenate(weights, axis=0)
    flat = returned[...].reshape(chips * requests, width)
    high = weights.astype(jnp.bfloat16)
    rest = weights - high.astype(jnp.float32)
    middle = rest.astype(jnp.bfloat16)
    low = (rest - middle.astype(jnp.float32)).astype(jnp.bfloat16)
    moe = dot(high, flat) + dot(middle, flat) + dot(low, flat)
    rows = [moe[j : j + 1] for j in range(requests)]
    moves = [jnp.broadcast_to(move[:, :1], (1, width)) for move in moves]
    is_odd = jnp.broadcast_to(odd[:, :1], (1, width)) == 1.0
    forward, backward = one_of(rows, moves, 1), one_of(rows, moves, 2)
    outer[...] = jnp.where(is_odd, forward, backward).astype(jnp.bfloat16)
    inner[...] = jnp.where(is_odd, backward, forward).astype(jnp.bfloat16)
    kept = [jnp.where(moves[j] == 0, rows[j], jnp.zeros_like(rows[j])) for j in range(requests)]
    stay[...] = jnp.concatenate(kept, axis=0).astype(jnp.bfloat16)


def in_vmem(count):
    return [pl.BlockSpec(memory_space=pltpu.VMEM) for _ in range(count)]


def in_smem(count):
    return [pl.BlockSpec(memory_space=pltpu.SMEM) for _ in range(count)]


SMALL = pltpu.CompilerParams(vmem_limit_bytes=6 * 1024 * 1024)
LIMIT = pltpu.CompilerParams(vmem_limit_bytes=10 * 1024 * 1024)


def body(
    latent_cache,
    page_table,
    lengths,
    move_to,
    query,
    hidden,
    norm_gain,
    expert_ids,
    expert_gates,
    gate_weight,
    up_weight,
    down_weight,
):
    pool = latent_cache[0, 0]
    table = page_table[0, 0]
    requests = table.shape[0]
    moves = move_to[0, 0]
    rows = hidden[0, 0]
    width = rows.shape[1]
    devices = lax.axis_size("ep")

    groups = lax.axis_size("grp")
    outer_pairs = [(i, (i + 1) % groups if i % 2 else (i - 1) % groups) for i in range(groups)]
    inner_pairs = [(i, i ^ 1) for i in range(groups)]

    def exchanged(outer, inner):
        return lax.ppermute(outer, "grp", outer_pairs), lax.ppermute(inner, "grp", inner_pairs)

    def served(stay, got_outer, got_inner):
        odd = mix[-2, 0] == 1.0
        from_prev = jnp.where(odd, got_inner, got_outer)
        from_next = jnp.where(odd, got_outer, got_inner)
        return jnp.concatenate([stay, from_prev, from_next], axis=0)[None, None]

    heads = query.shape[3]
    payload = jax.ShapeDtypeStruct((heads + BEHIND, VDIM), jnp.bfloat16)
    send_outer, send_inner, attn_stay, mix = pl.pallas_call(
        attend_kernel,
        out_shape=(
            payload,
            payload,
            jax.ShapeDtypeStruct((requests, heads, VDIM), jnp.bfloat16),
            jax.ShapeDtypeStruct((expert_ids.shape[2] + requests + 2, 128), jnp.float32),
        ),
        in_specs=in_smem(3) + in_vmem(4),
        out_specs=tuple(in_vmem(4)),
        compiler_params=SMALL,
        cost_estimate=pl.CostEstimate(flops=40_000_000_000, bytes_accessed=400_000_000, transcendentals=100_000_000),
    )(
        table, lengths[0, 0], moves, expert_ids[0, 0], expert_gates[0, 0], pool, query[0, 0]
    )

    cores = 2
    chips = devices // cores
    alike = [[cores * i + j for i in reversed(range(chips))] for j in range(cores)]
    count = chips * requests
    outgoing = pl.pallas_call(
        spread_kernel,
        out_shape=jax.ShapeDtypeStruct((chips, requests, width), jnp.bfloat16),
        in_specs=in_vmem(1),
        out_specs=in_vmem(1)[0],
        compiler_params=pltpu.CompilerParams(vmem_limit_bytes=2 * 1024 * 1024),
    )(rows)
    received = lax.all_to_all(
        outgoing, "ep", split_axis=0, concat_axis=0, axis_index_groups=alike, tiled=True
    )
    swap = [(i, i ^ 1) for i in range(devices)]
    weights = (gate_weight[0], up_weight[0], down_weight[0])
    traded = tuple(lax.ppermute(weight, "ep", swap) for weight in weights)
    received, send_outer, send_inner, attn_stay, mix = lax.optimization_barrier(
        (received, send_outer, send_inner, attn_stay, mix)
    )
    pair = pl.pallas_call(
        experts_kernel,
        out_shape=jax.ShapeDtypeStruct((chips, requests, width), jnp.bfloat16),
        in_specs=in_vmem(5) + [pl.BlockSpec(memory_space=pl.ANY) for _ in traded],
        out_specs=pl.BlockSpec(memory_space=pl.ANY),
        scratch_shapes=[pltpu.VMEM(weight.shape, weight.dtype) for weight in traded]
        + [pltpu.VMEM((PIECES, chips, requests, width // PIECES), jnp.bfloat16)]
        + [pltpu.SemaphoreType.DMA((len(traded),)), pltpu.SemaphoreType.DMA((PIECES,))],
        compiler_params=LIMIT,
    )(received, norm_gain[None, :], *weights, *traded)
    returned = lax.all_to_all(
        pair,
        "ep",
        split_axis=0,
        concat_axis=0,
        axis_index_groups=alike,
        tiled=True,
    )

    send_outer, send_inner, attn_stay, _ = lax.optimization_barrier(
        (send_outer, send_inner, attn_stay, pair)
    )
    got_outer, got_inner = exchanged(send_outer, send_inner)
    returned, got_outer, got_inner = lax.optimization_barrier((returned, got_outer, got_inner))
    line = jax.ShapeDtypeStruct((1, width), jnp.bfloat16)
    moe_outer, moe_inner, moe_stay = pl.pallas_call(
        functools.partial(gather_kernel, devices // SLICES),
        out_shape=(line, line, jax.ShapeDtypeStruct((requests, width), jnp.bfloat16)),
        in_specs=in_vmem(4),
        out_specs=tuple(in_vmem(3)),
        compiler_params=SMALL,
    )(returned, mix, got_outer, got_inner)
    return (
        served(attn_stay, got_outer[None, :heads], got_inner[None, :heads]),
        served(moe_stay, *exchanged(moe_outer, moe_inner)),
    )


def solution(mesh):
    in_specs = (
        P("grp", "ep", None, None, None),
        P("grp", "ep", None, None),
        P("grp", "ep", None),
        P("grp", "ep", None),
        P("grp", "ep", None, None, None),
        P("grp", "ep", None, None),
        P(),
        P("grp", "ep", None, None),
        P("grp", "ep", None, None),
        P("ep", None, None),
        P("ep", None, None),
        P("ep", None, None),
    )
    out_specs = (P("grp", "ep", None, None, None), P("grp", "ep", None, None))
    return jax.shard_map(body, mesh=mesh, in_specs=in_specs, out_specs=out_specs, check_vma=False)
```

```python
import functools

import jax
import jax.numpy as jnp
from jax import lax
from jax.experimental import pallas as pl
from jax.experimental.pallas import tpu as pltpu
from jax.sharding import PartitionSpec as P

VDIM = 512
QK_DIM = 192
SLICES = 8
BEHIND = 16
LAST = 1024


def dot(left, right):
    return jnp.dot(left, right, preferred_element_type=jnp.float32)


def one_of(choices, which, wanted):
    found = jnp.zeros_like(choices[0])
    for j, choice in enumerate(choices):
        found = jnp.where(which[j] == wanted, choice, found)
    return found


def spread_kernel(rows, out):
    out[...] = jnp.broadcast_to(rows[...][None], out.shape)


def attend_kernel(
    table, lens, moves, ids, gates, pool, query, outer, inner, stay, mix
):
    odd = lax.rem(lax.axis_index("grp"), 2)
    requests, heads = query.shape[0], query.shape[1]
    results = []
    for j in range(requests):
        keys = jnp.concatenate([pool[table[j, p]] for p in range(table.shape[1])], axis=0)
        scores = lax.dot_general(
            query[j], keys, (((1,), (1,)), ((), ())), preferred_element_type=jnp.float32
        ) * QK_DIM ** (-0.5)
        live = lax.broadcasted_iota(jnp.int32, scores.shape, 1) < lens[j]
        scores = jnp.where(live, scores, jnp.float32(-1e30))
        expo = jnp.exp(scores - jnp.max(scores, axis=1, keepdims=True))
        probs = (expo / jnp.sum(expo, axis=1, keepdims=True)).astype(jnp.bfloat16)
        results.append(dot(probs, keys[:, :VDIM]))
        stay[j] = jnp.where(moves[j] == 0, results[j], jnp.zeros_like(results[j])).astype(jnp.bfloat16)
    rows = ids.shape[0]
    lane = lax.broadcasted_iota(jnp.int32, (rows, mix.shape[1]), 1)
    total = jnp.zeros(lane.shape, jnp.float32)
    for k in range(ids.shape[1]):
        total = total + jnp.where(ids[:, k : k + 1] == lane, gates[:, k : k + 1], 0.0)
    mix[:rows] = total
    flags = [moves[j] for j in range(requests)] + [odd]
    place = lax.broadcasted_iota(jnp.int32, (mix.shape[0] - rows, mix.shape[1]), 0)
    kept = jnp.zeros(place.shape, jnp.int32)
    for j, flag in enumerate(flags):
        kept = jnp.where(place == j, flag, kept)
    mix[rows:] = kept.astype(jnp.float32)
    high = total.astype(jnp.bfloat16).astype(jnp.float32)
    middle = (total - high).astype(jnp.bfloat16).astype(jnp.float32)
    low = total - high - middle
    pieces = jnp.concatenate([high, middle, low, jnp.zeros_like(low)], axis=1)
    forward, backward = one_of(results, moves, 1), one_of(results, moves, 2)
    behind = outer.shape[0] - heads
    row_forward = jnp.broadcast_to(pieces[requests + 1 : requests + 2], (behind, pieces.shape[1]))
    row_backward = jnp.broadcast_to(pieces[requests : requests + 1], (behind, pieces.shape[1]))
    is_odd = odd == 1
    outer[:heads] = jnp.where(is_odd, forward, backward).astype(jnp.bfloat16)
    outer[heads:] = jnp.where(is_odd, row_forward, row_backward).astype(jnp.bfloat16)
    inner[:heads] = jnp.where(is_odd, backward, forward).astype(jnp.bfloat16)
    inner[heads:] = jnp.where(is_odd, row_backward, row_forward).astype(jnp.bfloat16)


def experts_kernel(
    x, gain, gate_a, up_a, down_a, gate_there, up_there, down_there, out, gate_b, up_b, down_b, large, small, sems, out_sems
):
    pairs = ((gate_there, gate_b), (up_there, up_b), (down_there, down_b))
    copies = [pltpu.make_async_copy(*pair, sems.at[i]) for i, pair in enumerate(pairs)]
    for copy in copies:
        copy.start()
    wide = x[...].reshape(x.shape[0] * x.shape[1], x.shape[2]).astype(jnp.float32)
    scale = lax.rsqrt(jnp.mean(wide * wide, axis=1, keepdims=True) + 1e-06)
    normed = (wide * scale * gain[...]).astype(jnp.bfloat16)
    act = (jax.nn.silu(dot(normed, gate_a[...])) * dot(normed, up_a[...])).astype(jnp.bfloat16)
    total = dot(act, down_a[...])
    copies[0].wait()
    gate = dot(normed, gate_b[...])
    copies[1].wait()
    act = (jax.nn.silu(gate) * dot(normed, up_b[...])).astype(jnp.bfloat16)
    copies[2].wait()
    leaving = []
    for i, (first, piece) in enumerate(((0, large), (large.shape[2], small))):
        columns = slice(first, first + piece.shape[2])
        values = total[:, columns] + dot(act, down_b[:, columns])
        piece[...] = values.astype(jnp.bfloat16).reshape(piece.shape)
        leaving.append(pltpu.make_async_copy(piece, out.at[:, :, columns], out_sems.at[i]))
        leaving[i].start()
    for copy in leaving:
        copy.wait()


def gather_kernel(experts, returned, mix, got_outer, got_inner, outer, inner, stay):
    chips, requests, width = returned.shape
    rows_served = mix.shape[0] - requests - 2
    moves = [mix[rows_served + j : rows_served + j + 1] for j in range(requests)]
    odd = mix[rows_served + requests : rows_served + requests + 1]
    is_odd = odd == 1.0
    heads = got_outer.shape[0] - BEHIND

    def mix_of(got):
        row = got[heads : heads + BEHIND].astype(jnp.float32)[:1]
        step = mix.shape[1]
        return row[:, :step] + row[:, step : 2 * step] + row[:, 2 * step : 3 * step]

    mix_outer, mix_inner = mix_of(got_outer), mix_of(got_inner)
    mix_next = jnp.where(is_odd, mix_outer, mix_inner)
    mix_prev = jnp.where(is_odd, mix_inner, mix_outer)
    lane = lax.broadcasted_iota(jnp.int32, (1, chips * requests), 1)
    weights = []
    for j in range(requests):
        own = mix[j : j + 1]
        home = jnp.where(moves[j] == 0, own, jnp.where(moves[j] == 1, mix_next, mix_prev))
        spread = jnp.zeros(lane.shape, jnp.float32)
        per_expert = chips * requests // experts
        for x in range(experts):
            spread = jnp.where(lane // per_expert == experts - 1 - x, home[:, x : x + 1], spread)
        weights.append(jnp.where(lane % requests == j, spread, 0.0))
    weights = jnp.concatenate(weights, axis=0)
    flat = returned[...].reshape(chips * requests, width)
    high = weights.astype(jnp.bfloat16)
    rest = weights - high.astype(jnp.float32)
    middle = rest.astype(jnp.bfloat16)
    low = (rest - middle.astype(jnp.float32)).astype(jnp.bfloat16)
    moe = dot(high, flat) + dot(middle, flat) + dot(low, flat)
    rows = [moe[j : j + 1] for j in range(requests)]
    moves = [jnp.broadcast_to(move[:, :1], (1, width)) for move in moves]
    is_odd = jnp.broadcast_to(odd[:, :1], (1, width)) == 1.0
    forward, backward = one_of(rows, moves, 1), one_of(rows, moves, 2)
    outer[...] = jnp.where(is_odd, forward, backward).astype(jnp.bfloat16)
    inner[...] = jnp.where(is_odd, backward, forward).astype(jnp.bfloat16)
    kept = [jnp.where(moves[j] == 0, rows[j], jnp.zeros_like(rows[j])) for j in range(requests)]
    stay[...] = jnp.concatenate(kept, axis=0).astype(jnp.bfloat16)


def in_vmem(count):
    return [pl.BlockSpec(memory_space=pltpu.VMEM) for _ in range(count)]


def in_smem(count):
    return [pl.BlockSpec(memory_space=pltpu.SMEM) for _ in range(count)]


SMALL = pltpu.CompilerParams(vmem_limit_bytes=6 * 1024 * 1024)
LIMIT = pltpu.CompilerParams(vmem_limit_bytes=10 * 1024 * 1024)


def body(
    latent_cache,
    page_table,
    lengths,
    move_to,
    query,
    hidden,
    norm_gain,
    expert_ids,
    expert_gates,
    gate_weight,
    up_weight,
    down_weight,
):
    pool = latent_cache[0, 0]
    table = page_table[0, 0]
    requests = table.shape[0]
    moves = move_to[0, 0]
    rows = hidden[0, 0]
    width = rows.shape[1]
    devices = lax.axis_size("ep")

    groups = lax.axis_size("grp")
    outer_pairs = [(i, (i + 1) % groups if i % 2 else (i - 1) % groups) for i in range(groups)]
    inner_pairs = [(i, i ^ 1) for i in range(groups)]

    def exchanged(outer, inner):
        return lax.ppermute(outer, "grp", outer_pairs), lax.ppermute(inner, "grp", inner_pairs)

    def served(stay, got_outer, got_inner):
        odd = mix[-2, 0] == 1.0
        from_prev = jnp.where(odd, got_inner, got_outer)
        from_next = jnp.where(odd, got_outer, got_inner)
        return jnp.concatenate([stay, from_prev, from_next], axis=0)[None, None]

    heads = query.shape[3]
    payload = jax.ShapeDtypeStruct((heads + BEHIND, VDIM), jnp.bfloat16)
    send_outer, send_inner, attn_stay, mix = pl.pallas_call(
        attend_kernel,
        out_shape=(
            payload,
            payload,
            jax.ShapeDtypeStruct((requests, heads, VDIM), jnp.bfloat16),
            jax.ShapeDtypeStruct((expert_ids.shape[2] + requests + 2, 128), jnp.float32),
        ),
        in_specs=in_smem(3) + in_vmem(4),
        out_specs=tuple(in_vmem(4)),
        compiler_params=SMALL,
        cost_estimate=pl.CostEstimate(flops=40_000_000_000, bytes_accessed=400_000_000, transcendentals=100_000_000),
    )(
        table, lengths[0, 0], moves, expert_ids[0, 0], expert_gates[0, 0], pool, query[0, 0]
    )

    cores = 2
    chips = devices // cores
    alike = [[cores * i + j for i in reversed(range(chips))] for j in range(cores)]
    count = chips * requests
    outgoing = pl.pallas_call(
        spread_kernel,
        out_shape=jax.ShapeDtypeStruct((chips, requests, width), jnp.bfloat16),
        in_specs=in_vmem(1),
        out_specs=in_vmem(1)[0],
        compiler_params=pltpu.CompilerParams(vmem_limit_bytes=2 * 1024 * 1024),
    )(rows)
    received = lax.all_to_all(
        outgoing, "ep", split_axis=0, concat_axis=0, axis_index_groups=alike, tiled=True
    )
    swap = [(i, i ^ 1) for i in range(devices)]
    weights = (gate_weight[0], up_weight[0], down_weight[0])
    traded = tuple(lax.ppermute(weight, "ep", swap) for weight in weights)
    received, send_outer, send_inner, attn_stay, mix = lax.optimization_barrier(
        (received, send_outer, send_inner, attn_stay, mix)
    )
    pair = pl.pallas_call(
        experts_kernel,
        out_shape=jax.ShapeDtypeStruct((chips, requests, width), jnp.bfloat16),
        in_specs=in_vmem(5) + [pl.BlockSpec(memory_space=pl.ANY) for _ in traded],
        out_specs=pl.BlockSpec(memory_space=pl.ANY),
        scratch_shapes=[pltpu.VMEM(weight.shape, weight.dtype) for weight in traded]
        + [pltpu.VMEM((chips, requests, part), jnp.bfloat16) for part in (width - LAST, LAST)]
        + [pltpu.SemaphoreType.DMA((len(traded),)), pltpu.SemaphoreType.DMA((2,))],
        compiler_params=LIMIT,
    )(received, norm_gain[None, :], *weights, *traded)
    returned = lax.all_to_all(
        pair,
        "ep",
        split_axis=0,
        concat_axis=0,
        axis_index_groups=alike,
        tiled=True,
    )

    send_outer, send_inner, attn_stay, _ = lax.optimization_barrier(
        (send_outer, send_inner, attn_stay, pair)
    )
    got_outer, got_inner = exchanged(send_outer, send_inner)
    returned, got_outer, got_inner = lax.optimization_barrier((returned, got_outer, got_inner))
    line = jax.ShapeDtypeStruct((1, width), jnp.bfloat16)
    moe_outer, moe_inner, moe_stay = pl.pallas_call(
        functools.partial(gather_kernel, devices // SLICES),
        out_shape=(line, line, jax.ShapeDtypeStruct((requests, width), jnp.bfloat16)),
        in_specs=in_vmem(4),
        out_specs=tuple(in_vmem(3)),
        compiler_params=SMALL,
    )(returned, mix, got_outer, got_inner)
    return (
        served(attn_stay, got_outer[None, :heads], got_inner[None, :heads]),
        served(moe_stay, *exchanged(moe_outer, moe_inner)),
    )


def solution(mesh):
    in_specs = (
        P("grp", "ep", None, None, None),
        P("grp", "ep", None, None),
        P("grp", "ep", None),
        P("grp", "ep", None),
        P("grp", "ep", None, None, None),
        P("grp", "ep", None, None),
        P(),
        P("grp", "ep", None, None),
        P("grp", "ep", None, None),
        P("ep", None, None),
        P("ep", None, None),
        P("ep", None, None),
    )
    out_specs = (P("grp", "ep", None, None, None), P("grp", "ep", None, None))
    return jax.shard_map(body, mesh=mesh, in_specs=in_specs, out_specs=out_specs, check_vma=False)
```
